512 devices in a mesh: tm: 16 (over z_lo, core), space: 32 (over z_hi, y, x).
Axes of the slice: x: 4, y: 4, z: 16 (z_hi: 2, z_lo: 8; z = z_hi * 8 + z_lo), core: 2. Of those that a mesh axis runs over, the one named last changes fastest.
Arguments:
- forcing: float32 [2, 16, 8, 32, 4096], P(None, 'tm', None, None, 'space'), may hold values from -6 to 6
- wind_x: float32 [16, 2, 8, 32, 4096], P('tm', None, None, None, 'space'), may hold values from -1 to 1
- wind_y: float32 [16, 2, 8, 32, 4096], P('tm', None, None, None, 'space'), may hold values from -1 to 1
Outputs:
- adjoint: float32 [2, 16, 8, 32, 4096], P(None, 'tm', None, None, 'space')
The draws below stay inside these ranges and needn't reach their ends.
All inputs are finite; a program needn't handle non-finite values.
Results may differ from the reference program's by a relative error of at most 0.00015.
Values sent between devices are 32-bit elements; how exact they have to be, the bound alone decides.
No kernel may reach another device: no remote copies, remote signals or barrier semaphores. Data moves between devices by JAX's collectives and lax.ppermute only.
A program may use at most 64 MiB of HBM per device.

```python
import jax
import jax.numpy as jnp
import numpy as np
from jax import lax

LEV = 8
STEPS = 2
MEMBERS = 2
WINDOWS = 16
ROWS = 32
NX = 4096


def shard_levels(own_key, dims, cuts, least, high):
    def one(axis_at, shards_of):
        steps = jax.random.uniform(jax.random.fold_in(jax.random.fold_in(own_key, 6), axis_at), (shards_of,), jnp.float32, least / len(cuts), high / len(cuts))
        return jnp.repeat(jnp.exp(steps), dims[axis_at] // shards_of).reshape((-1,) + (1,) * (len(dims) - axis_at - 1))

    gain = one(*cuts[0])
    for cut in cuts[1:]:
        gain = gain * one(*cut)
    return gain


def centred(rng, dims, scale, limit, shards=(), kind=jnp.bfloat16):
    result = jax.random.normal(rng, dims, jnp.float32) * scale
    if len(shards) > 0:
        result = shard_levels(rng, dims, shards, -0.22, 0.18) * result
    return jnp.clip(result, min=-limit, max=limit).astype(kind)


def setup_inputs(seed: int = 0) -> dict:
    seeds = jax.random.split(jax.random.key(seed), 4)
    return {
        "forcing": centred(seeds[0], (MEMBERS, WINDOWS, LEV, ROWS, NX), 1.0, 6.0, ((1, 16), (4, 32)), jnp.float32),
        "wind_x": jnp.clip(jax.random.uniform(seeds[1], (WINDOWS, STEPS, LEV, ROWS, NX), jnp.float32, -1.0, 1.0) * shard_levels(seeds[1], (WINDOWS, STEPS, LEV, ROWS, NX), ((0, 16), (4, 32)), -0.4, 0.0), -1.0, 1.0),
        "wind_y": jnp.clip(jax.random.uniform(seeds[2], (WINDOWS, STEPS, LEV, ROWS, NX), jnp.float32, -1.0, 1.0) * shard_levels(seeds[2], (WINDOWS, STEPS, LEV, ROWS, NX), ((0, 16), (4, 32)), -0.4, 0.0), -1.0, 1.0),
    }


time_step = 0.01
lobatto_points = [-1.0, -0.8717401485096066153, -0.5917001814331423021, -0.2092992179024788688, 0.2092992179024788688, 0.5917001814331423021, 0.8717401485096066153, 1.0]


def legendre_seven(point):
    before = 1.0
    current = point
    for order in range(1, 7):
        before, current = current, ((2 * order + 1) * point * current - order * before) / (order + 1)
    return current


def lobatto_table():
    values = [legendre_seven(point) for point in lobatto_points]
    table = np.zeros((8, 8))
    for row_index in range(8):
        for col_index in range(8):
            if row_index != col_index:
                table[row_index, col_index] = values[row_index] / (values[col_index] * (lobatto_points[row_index] - lobatto_points[col_index]))
    table[0, 0] = -14.0
    table[7, 7] = 14.0
    return table.astype(np.float32)


def average_pairs(values, west_edge, east_edge):
    shaped = values.reshape(values.shape[:-1] + (-1, 8))
    firsts = shaped[..., :, 0]
    lasts = shaped[..., :, 7]
    before = jnp.concatenate([west_edge[..., None], lasts[..., :-1]], -1)
    after = jnp.concatenate([firsts[..., 1:], east_edge[..., None]], -1)
    shaped = shaped.at[..., :, 0].set(0.5 * (firsts + before))
    shaped = shaped.at[..., :, 7].set(0.5 * (lasts + after))
    return shaped.reshape(values.shape)


def adjoint_step(field, winds_x, winds_y, table):
    field = average_pairs(field, field[..., -1], field[..., 0])
    swapped = jnp.swapaxes(field, -1, -2)
    swapped = average_pairs(swapped, swapped[..., 0], swapped[..., -1])
    field = jnp.swapaxes(swapped, -1, -2)
    flux_x = (winds_x * field).reshape(field.shape[:-1] + (-1, 8))
    grad_x = jnp.einsum('...ei,ij->...ej', flux_x, table, precision=lax.Precision.HIGHEST).reshape(field.shape)
    flux_y = (winds_y * field).reshape(field.shape[:-2] + (-1, 8, field.shape[-1]))
    grad_y = jnp.einsum('...eix,ij->...ejx', flux_y, table, precision=lax.Precision.HIGHEST).reshape(field.shape)
    return field - time_step * (grad_x + grad_y)


def reference(forcing, wind_x, wind_y):
    table = jnp.asarray(lobatto_table()).astype(forcing.dtype)
    current = forcing[:, WINDOWS - 1]
    results = [current]
    for window in range(WINDOWS - 2, -1, -1):
        carried = current
        for substep in range(STEPS - 1, -1, -1):
            carried = adjoint_step(carried, wind_x[window + 1, substep], wind_y[window + 1, substep], table)
        current = forcing[:, window] + carried
        results.append(current)
    return jnp.stack(results[::-1], axis=1)
```

```python
import functools

import jax
import jax.numpy as jnp
import numpy as np
from jax import lax
from jax.experimental import pallas as pl
from jax.experimental.pallas import tpu as pltpu
from jax.sharding import PartitionSpec as P

time_step = 0.01
lobatto_points = [
    -1.0,
    -0.8717401485096066,
    -0.5917001814331423,
    -0.20929921790247888,
    0.20929921790247888,
    0.5917001814331423,
    0.8717401485096066,
    1.0,
]


def legendre_seven(point):
    before = 1.0
    current = point
    for order in range(1, 7):
        before, current = (
            current,
            ((2 * order + 1) * point * current - order * before) / (order + 1),
        )
    return current


def lobatto_table():
    values = [legendre_seven(point) for point in lobatto_points]
    table = np.zeros((8, 8))
    for row_index in range(8):
        for col_index in range(8):
            if row_index != col_index:
                table[row_index, col_index] = values[row_index] / (
                    values[col_index] * (lobatto_points[row_index] - lobatto_points[col_index])
                )
    table[0, 0] = -14.0
    table[7, 7] = 14.0
    return table.astype(np.float32)


def adjoint_steps(own_ref, west_ref, east_ref, dx_ref, dy_ref, start, windows, emit, last_moves):
    members = 2
    rows = own_ref.shape[2]
    width = own_ref.shape[3]
    shape = (members * rows, 3 * width)
    row = lax.broadcasted_iota(jnp.int32, shape, 0)
    col = lax.broadcasted_iota(jnp.int32, shape, 1)
    from_west = (col % 8) == 0
    from_east = (col % 8) == 7
    from_above = ((row % 8) == 0) & ((row % rows) != 0)
    from_below = ((row % 8) == 7) & ((row % rows) != rows - 1)
    high = lax.Precision.HIGHEST

    def wide(window, index):
        return jnp.concatenate(
            [west_ref[window, index], own_ref[window, index], east_ref[window, index]], axis=1
        )

    moved = start
    for window in range(windows - 1, -1, -1):
        field = jnp.concatenate([wide(window, 4), wide(window, 5)], axis=0)
        if moved is not None:
            field = field + moved
        emit(window, field[:, width : 2 * width])
        if window == 0 and not last_moves:
            return None
        for substep in (1, 0):
            wx = wide(window, substep)
            wy = wide(window, 2 + substep)
            wx = jnp.concatenate([wx, wx], axis=0)
            wy = jnp.concatenate([wy, wy], axis=0)
            partner = jnp.where(
                from_west,
                pltpu.roll(field, 1, 1),
                jnp.where(from_east, pltpu.roll(field, 3 * width - 1, 1), field),
            )
            q = 0.5 * (field + partner)
            partner = jnp.where(
                from_above,
                pltpu.roll(q, 1, 0),
                jnp.where(from_below, pltpu.roll(q, members * rows - 1, 0), q),
            )
            q = 0.5 * (q + partner)
            u = wx * q
            stacked = jnp.concatenate(
                [u[:, :width], u[:, width : 2 * width], u[:, 2 * width :]], axis=0
            )
            gx = jnp.dot(
                stacked, dx_ref[...], precision=high, preferred_element_type=jnp.float32
            )
            n = members * rows
            gx = jnp.concatenate([gx[:n], gx[n : 2 * n], gx[2 * n :]], axis=1)
            gy = jnp.dot(
                dy_ref[...], wy * q, precision=high, preferred_element_type=jnp.float32
            )
            field = q - (gx + gy)
        moved = field
    return moved


def first_kernel(own_ref, west_ref, east_ref, dx_ref, dy_ref, out_ref):
    width = own_ref.shape[3]
    moved = adjoint_steps(
        own_ref, west_ref, east_ref, dx_ref, dy_ref, None, own_ref.shape[0], lambda w, v: None, True
    )
    out_ref[...] = moved[:, width : 2 * width]


def second_kernel(own_ref, west_ref, east_ref, dx_ref, dy_ref, pw_ref, pc_ref, pe_ref, out_ref):
    rows = own_ref.shape[2]

    def emit(window, field):
        out_ref[window, 0] = field[:rows]
        out_ref[window, 1] = field[rows:]

    start = jnp.concatenate([pw_ref[...], pc_ref[...], pe_ref[...]], axis=1)
    adjoint_steps(
        own_ref, west_ref, east_ref, dx_ref, dy_ref, start, own_ref.shape[0], emit, False
    )


def local_call(kernel, out_shape, count):
    return pl.pallas_call(
        kernel,
        out_shape=out_shape,
        in_specs=[pl.BlockSpec(memory_space=pltpu.VMEM)] * count,
        out_specs=pl.BlockSpec(memory_space=pltpu.VMEM),
        compiler_params=pltpu.CompilerParams(vmem_limit_bytes=32 * 1024 * 1024),
    )


def on_device(forcing, wind_x, wind_y):
    members, _, levels, rows, width = forcing.shape
    steps = wind_x.shape[1]
    tm = lax.axis_size("tm")
    space = lax.axis_size("space")
    group = levels
    groups = [list(range(i, i + group)) for i in range(0, tm, group)]

    def flat(t, s):
        return t * space + s % space

    def moved_by(block, dt, ds):
        pairs = [
            (flat(t, s), flat(t + dt, s + ds))
            for t in range(tm)
            for s in range(space)
            if 0 <= t + dt < tm
        ]
        return lax.ppermute(block, ("tm", "space"), pairs)

    packed = jnp.concatenate([wind_x[0], wind_y[0], forcing[:, 0]], axis=0)
    packed = jnp.swapaxes(packed, 0, 1)
    own = lax.all_to_all(packed, "tm", 0, 0, axis_index_groups=groups, tiled=True)
    west = moved_by(own, 0, 1)
    east = moved_by(own, 0, -1)

    table = lobatto_table() * np.float32(time_step)
    dx = jnp.asarray(np.kron(np.eye(width // 8, dtype=np.float32), table))
    dy = jnp.asarray(np.kron(np.eye(members * rows // 8, dtype=np.float32), table.T))

    flat_field = jax.ShapeDtypeStruct((members * rows, width), jnp.float32)
    sent = local_call(first_kernel, flat_field, 5)(own, west, east, dx, dy)
    below = moved_by(sent, -group, 0)
    below_west = moved_by(sent, -group, 1)
    below_east = moved_by(sent, -group, -1)
    result = local_call(
        second_kernel, jax.ShapeDtypeStruct((group, members, rows, width), jnp.float32), 8
    )(own, west, east, dx, dy, below_west, below, below_east)
    result = lax.all_to_all(result, "tm", 0, 0, axis_index_groups=groups, tiled=True)
    return jnp.swapaxes(result, 0, 1)[:, None]


def solution(mesh):
    placed = (
        P(None, "tm", None, None, "space"),
        P("tm", None, None, None, "space"),
        P("tm", None, None, None, "space"),
    )
    return jax.shard_map(
        on_device,
        mesh=mesh,
        in_specs=placed,
        out_specs=P(None, "tm", None, None, "space"),
        check_vma=False,
    )
```

```python
import jax
import jax.numpy as jnp
import numpy as np
from jax import lax
from jax.experimental import pallas as pl
from jax.experimental.pallas import tpu as pltpu
from jax.sharding import PartitionSpec as P

time_step = 0.01
lobatto_points = [
    -1.0,
    -0.8717401485096066,
    -0.5917001814331423,
    -0.20929921790247888,
    0.20929921790247888,
    0.5917001814331423,
    0.8717401485096066,
    1.0,
]


def legendre_seven(point):
    before = 1.0
    current = point
    for order in range(1, 7):
        before, current = (
            current,
            ((2 * order + 1) * point * current - order * before) / (order + 1),
        )
    return current


def lobatto_table():
    values = [legendre_seven(point) for point in lobatto_points]
    table = np.zeros((8, 8))
    for row_index in range(8):
        for col_index in range(8):
            if row_index != col_index:
                table[row_index, col_index] = values[row_index] / (
                    values[col_index] * (lobatto_points[row_index] - lobatto_points[col_index])
                )
    table[0, 0] = -14.0
    table[7, 7] = 14.0
    return table.astype(np.float32)


def pair_tiles(windows):
    last = 2 * windows
    tiles = []

    def block(step, kind):
        return (windows - 1 - (step - 1) // 2, 2 * kind + (step % 2))

    for step in range(1, windows + 1):
        for kind in (0, 1):
            tiles.append((block(step, kind), block(last + 1 - step, kind), 8 * (last - step)))
    tiles.append(((windows - 1, 4), None, 16 * windows))
    tiles.append(((windows - 1, 5), None, 16 * windows))
    for window in range(windows - 2, windows // 2 - 1, -1):
        for member in (4, 5):
            tiles.append(
                ((window, member), (windows - 2 - window, member), 16 * (window + 1))
            )
    middle = windows // 2 - 1
    tiles.append(((middle, 4), (middle, 5), 16 * (middle + 1)))
    return tiles


def places(windows):
    found = {}
    for index, (first, second, columns) in enumerate(pair_tiles(windows)):
        found[first] = (index, 0)
        if second is not None:
            found[second] = (index, columns)
    return found


def pack_kernel(own_ref, even_ref, odd_ref):
    windows, _, rows, width = own_ref.shape
    col = lax.broadcasted_iota(jnp.int32, (rows, width), 1)
    odd_place = lax.axis_index("space") % 2

    def write(low_ref, high_ref):
        for index, (first, second, columns) in enumerate(pair_tiles(windows)):
            one = own_ref[first[0], first[1]]
            if second is None:
                low_ref[index] = one
                high_ref[index] = one
                continue
            other = own_ref[second[0], second[1]]
            low_ref[index] = jnp.where(col < columns, one, pltpu.roll(other, columns, 1))
            high_ref[index] = jnp.where(
                col >= width - columns, one, pltpu.roll(other, width - columns, 1)
            )

    @pl.when(odd_place == 0)
    def _():
        write(odd_ref, even_ref)

    @pl.when(odd_place == 1)
    def _():
        write(even_ref, odd_ref)


def adjoint_steps(own_ref, halo, dx_ref, dy_ref, start, emit, last_moves):
    windows, _, rows, width = own_ref.shape
    members = 2
    shape = (members * rows, 3 * width)
    row = lax.broadcasted_iota(jnp.int32, shape, 0)
    col = lax.broadcasted_iota(jnp.int32, shape, 1)
    from_west = (col % 8) == 0
    from_east = (col % 8) == 7
    from_above = ((row % 8) == 0) & ((row % rows) != 0)
    from_below = ((row % 8) == 7) & ((row % rows) != rows - 1)
    high = lax.Precision.HIGHEST

    def wide(window, index):
        west, east = halo(window, index)
        return jnp.concatenate([west, own_ref[window, index], east], axis=1)

    moved = start
    for window in range(windows - 1, -1, -1):
        field = jnp.concatenate([wide(window, 4), wide(window, 5)], axis=0)
        if moved is not None:
            field = field + moved
        emit(window, field[:, width : 2 * width])
        if window == 0 and not last_moves:
            return None
        for substep in (1, 0):
            wx = wide(window, substep)
            wy = wide(window, 2 + substep)
            wx = jnp.concatenate([wx, wx], axis=0)
            wy = jnp.concatenate([wy, wy], axis=0)
            partner = jnp.where(
                from_west,
                pltpu.roll(field, 1, 1),
                jnp.where(from_east, pltpu.roll(field, 3 * width - 1, 1), field),
            )
            q = 0.5 * (field + partner)
            partner = jnp.where(
                from_above,
                pltpu.roll(q, 1, 0),
                jnp.where(from_below, pltpu.roll(q, members * rows - 1, 0), q),
            )
            q = 0.5 * (q + partner)
            u = wx * q
            stacked = jnp.concatenate(
                [u[:, :width], u[:, width : 2 * width], u[:, 2 * width :]], axis=0
            )
            gx = jnp.dot(
                stacked, dx_ref[...], precision=high, preferred_element_type=jnp.float32
            )
            n = members * rows
            gx = jnp.concatenate([gx[:n], gx[n : 2 * n], gx[2 * n :]], axis=1)
            gy = jnp.dot(
                dy_ref[...], wy * q, precision=high, preferred_element_type=jnp.float32
            )
            field = q - (gx + gy)
        moved = field
    return moved


def halo_reader(windows, width, even_ref, odd_ref, far_ref):
    found = places(windows)
    odd_place = lax.axis_index("space") % 2 == 1

    def read(window, index):
        tile, shift = found[(window, index)]
        by_even = even_ref[tile]
        by_odd = odd_ref[tile] + far_ref[tile]
        west = jnp.where(odd_place, by_even, by_odd)
        east = jnp.where(odd_place, by_odd, by_even)
        if shift:
            west = pltpu.roll(west, shift, 1)
            east = pltpu.roll(east, width - shift, 1)
        return west, east

    return read


def emit_to(out_ref):
    rows = out_ref.shape[2]

    def emit(window, field):
        out_ref[window, 0] = field[:rows]
        out_ref[window, 1] = field[rows:]

    return emit


def upper_kernel(own_ref, even_ref, odd_ref, far_ref, dx_ref, dy_ref, out_ref, sent_ref):
    windows, _, _, width = own_ref.shape

    @pl.when(lax.axis_index("tm") >= windows)
    def _():
        halo = halo_reader(windows, width, even_ref, odd_ref, far_ref)
        moved = adjoint_steps(own_ref, halo, dx_ref, dy_ref, None, emit_to(out_ref), True)
        sent_ref[...] = moved[:, width : 2 * width]


def lower_kernel(
    done_ref, own_ref, even_ref, odd_ref, far_ref, dx_ref, dy_ref, here_ref, pe_ref, po_ref, out_ref
):
    windows, _, _, width = own_ref.shape

    @pl.when(lax.axis_index("tm") < windows)
    def _():
        halo = halo_reader(windows, width, even_ref, odd_ref, far_ref)
        odd_place = lax.axis_index("space") % 2 == 1
        by_even = pe_ref[...]
        by_odd = po_ref[...]
        west = jnp.where(odd_place, by_even, by_odd)
        east = jnp.where(odd_place, by_odd, by_even)
        start = jnp.concatenate([west, here_ref[...], east], axis=1)
        adjoint_steps(own_ref, halo, dx_ref, dy_ref, start, emit_to(out_ref), False)


def local_call(kernel, out_shape, count, aliases=None):
    whole = pl.BlockSpec(memory_space=pltpu.VMEM)
    return pl.pallas_call(
        kernel,
        out_shape=out_shape,
        in_specs=[whole] * count,
        out_specs=jax.tree.map(lambda _: whole, out_shape),
        input_output_aliases=aliases or {},
        compiler_params=pltpu.CompilerParams(vmem_limit_bytes=32 * 1024 * 1024),
    )


def on_device(forcing, wind_x, wind_y):
    members, _, levels, rows, width = forcing.shape
    tm = lax.axis_size("tm")
    space = lax.axis_size("space")
    group = levels
    groups = [list(range(i, i + group)) for i in range(0, tm, group)]
    layer = space // 2

    def even_mate(s):
        return s ^ 1

    def odd_mate(s):
        return (s + 1) % space if s % 2 else (s - 1) % space

    def is_far(s):
        return s % layer in (0, layer - 1)

    def exchange(block, mate, times=range(tm), places_of=range(space), dt=0):
        pairs = [
            (t * space + s, (t + dt) * space + mate(s)) for t in times for s in places_of
        ]
        return lax.ppermute(block, ("tm", "space"), pairs)

    near = [s for s in range(space) if not is_far(s)]
    far = [s for s in range(space) if is_far(s)]
    upper = range(group, tm)
    lower = range(group)

    packed = jnp.concatenate([wind_x[0], wind_y[0], forcing[:, 0]], axis=0)
    packed = jnp.swapaxes(packed, 0, 1)
    own = lax.all_to_all(packed, "tm", 0, 0, axis_index_groups=groups, tiled=True)

    tiles = jax.ShapeDtypeStruct((len(pair_tiles(group)), rows, width), jnp.float32)
    to_even, to_odd = local_call(pack_kernel, (tiles, tiles), 1)(own)
    far_upper = exchange(to_odd, odd_mate, upper, far)
    even = exchange(to_even, even_mate)
    odd = exchange(to_odd, odd_mate, places_of=near)
    to_odd_later = to_odd + 0.0 * (even[0, 0, 0] + odd[0, 0, 0])
    far_lower = exchange(to_odd_later, odd_mate, lower, far)

    table = lobatto_table() * np.float32(time_step)
    dx = jnp.asarray(np.kron(np.eye(width // 8, dtype=np.float32), table))
    dy = jnp.asarray(np.kron(np.eye(members * rows // 8, dtype=np.float32), table.T))

    result_shape = jax.ShapeDtypeStruct((group, members, rows, width), jnp.float32)
    flat_field = jax.ShapeDtypeStruct((members * rows, width), jnp.float32)
    done, sent = local_call(upper_kernel, (result_shape, flat_field), 6)(
        own, even, odd, far_upper, dx, dy
    )
    from_here = exchange(sent, lambda s: s, upper, dt=-group)
    from_even = exchange(sent, even_mate, upper, dt=-group)
    from_odd = exchange(sent, odd_mate, upper, dt=-group)
    result = local_call(lower_kernel, result_shape, 10, {0: 0})(
        done, own, even, odd, far_lower, dx, dy, from_here, from_even, from_odd
    )
    result = lax.all_to_all(result, "tm", 0, 0, axis_index_groups=groups, tiled=True)
    return jnp.swapaxes(result, 0, 1)[:, None]


def solution(mesh):
    placed = (
        P(None, "tm", None, None, "space"),
        P("tm", None, None, None, "space"),
        P("tm", None, None, None, "space"),
    )
    return jax.shard_map(
        on_device,
        mesh=mesh,
        in_specs=placed,
        out_specs=P(None, "tm", None, None, "space"),
        check_vma=False,
    )
```

```python
import jax
import jax.numpy as jnp
import numpy as np
from jax import lax
from jax.experimental import pallas as pl
from jax.experimental.pallas import tpu as pltpu
from jax.sharding import PartitionSpec as P

time_step = 0.01
lobatto_points = [
    -1.0,
    -0.8717401485096066,
    -0.5917001814331423,
    -0.20929921790247888,
    0.20929921790247888,
    0.5917001814331423,
    0.8717401485096066,
    1.0,
]


def legendre_seven(point):
    before = 1.0
    current = point
    for order in range(1, 7):
        before, current = (
            current,
            ((2 * order + 1) * point * current - order * before) / (order + 1),
        )
    return current


def lobatto_table():
    values = [legendre_seven(point) for point in lobatto_points]
    table = np.zeros((8, 8))
    for row_index in range(8):
        for col_index in range(8):
            if row_index != col_index:
                table[row_index, col_index] = values[row_index] / (
                    values[col_index] * (lobatto_points[row_index] - lobatto_points[col_index])
                )
    table[0, 0] = -14.0
    table[7, 7] = 14.0
    return table.astype(np.float32)


def split_bf16(value):
    high = value.astype(jnp.bfloat16)
    return high, (value - high.astype(jnp.float32)).astype(jnp.bfloat16)


def derivative_tables(width):
    table = lobatto_table() * np.float32(time_step)
    along_x = np.kron(np.eye(width // 8, dtype=np.float32), table)
    high = along_x.astype(jnp.bfloat16)
    low = (along_x - high.astype(np.float32)).astype(jnp.bfloat16)
    product = np.zeros((2 * width, 2 * width), jnp.bfloat16)
    product[:width, :width] = high
    product[width:, :width] = high
    product[:width, width:] = low
    along_y = np.zeros((8, 8, width), np.float32)
    for shift in range(8):
        for node in range(8):
            along_y[shift, node, :] = table[(node - shift) % 8, node]
    return jnp.asarray(product), jnp.asarray(along_y)


def pair_tiles(windows):
    last = 2 * windows
    tiles = []

    def block(step, kind):
        return (windows - 1 - (step - 1) // 2, 2 * kind + (step % 2))

    for step in range(1, windows + 1):
        for kind in (0, 1):
            tiles.append((block(step, kind), block(last + 1 - step, kind), 8 * (last - step)))
    tiles.append(((windows - 1, 4), None, 16 * windows))
    tiles.append(((windows - 1, 5), None, 16 * windows))
    for window in range(windows - 2, windows // 2 - 1, -1):
        for member in (4, 5):
            tiles.append(
                ((window, member), (windows - 2 - window, member), 16 * (window + 1))
            )
    middle = windows // 2 - 1
    tiles.append(((middle, 4), (middle, 5), 16 * (middle + 1)))
    return tiles


def places(windows):
    found = {}
    for index, (first, second, columns) in enumerate(pair_tiles(windows)):
        found[first] = (index, 0)
        if second is not None:
            found[second] = (index, columns)
    return found


def layer_here():
    return lax.axis_index("space") // (lax.axis_size("space") // 2)


def gather_kernel(wind_x_ref, wind_y_ref, forcing_ref, out_ref, sems):
    levels = out_ref.shape[0]
    half = levels // 2
    layer = layer_here()
    copies = []
    for part in (0, 1):
        here = pl.ds(half * part, half)
        there = pl.ds(half * jnp.bitwise_xor(layer, part), half)
        for index in (0, 1):
            copies.append((wind_x_ref.at[0, index, here], out_ref.at[there, index]))
            copies.append((wind_y_ref.at[0, index, here], out_ref.at[there, 2 + index]))
            copies.append((forcing_ref.at[index, 0, here], out_ref.at[there, 4 + index]))
    copies = [
        pltpu.make_async_copy(source, target, sems.at[index])
        for index, (source, target) in enumerate(copies)
    ]
    for copy in copies:
        copy.start()
    for copy in copies:
        copy.wait()


def scatter_kernel(in_ref, out_ref, sems):
    levels = in_ref.shape[0]
    half = levels // 2
    layer = layer_here()
    copies = []
    for part in (0, 1):
        here = pl.ds(half * part, half)
        there = pl.ds(half * jnp.bitwise_xor(layer, part), half)
        for member in (0, 1):
            copies.append(
                pltpu.make_async_copy(
                    in_ref.at[there, member],
                    out_ref.at[member, 0, here],
                    sems.at[2 * part + member],
                )
            )
    for copy in copies:
        copy.start()
    for copy in copies:
        copy.wait()


def pack_kernel(own_ref, even_ref, odd_ref):
    windows, _, rows, width = own_ref.shape
    col = lax.broadcasted_iota(jnp.int32, (rows, width), 1)
    odd_place = lax.axis_index("space") % 2

    def write(low_ref, high_ref):
        for index, (first, second, columns) in enumerate(pair_tiles(windows)):
            one = own_ref[first[0], first[1]]
            if second is None:
                low_ref[index] = one
                high_ref[index] = one
                continue
            other = own_ref[second[0], second[1]]
            low_ref[index] = jnp.where(col < columns, one, pltpu.roll(other, columns, 1))
            high_ref[index] = jnp.where(
                col >= width - columns, one, pltpu.roll(other, width - columns, 1)
            )

    @pl.when(odd_place == 0)
    def _():
        write(odd_ref, even_ref)

    @pl.when(odd_place == 1)
    def _():
        write(even_ref, odd_ref)


def shift_tiles(tiles, distance):
    distance %= tiles.shape[0]
    return jnp.concatenate([tiles[-distance:], tiles[:-distance]], axis=0)


def roll_columns(value, distance):
    width = value.shape[-1]
    return pltpu.roll(value.reshape(-1, width), distance % width, 1).reshape(value.shape)


def roll_nodes(value, distance):
    width = value.shape[-1]
    return pltpu.roll(value.reshape(-1, 8, width), distance % 8, 1).reshape(value.shape)


def adjoint_step(field, wind_x, wind_y, along_x, along_y):
    count, blocks, _, width = field.shape
    elements = blocks // 2
    col = lax.broadcasted_iota(jnp.int32, (1, 1, 8, width), 3)
    node = lax.broadcasted_iota(jnp.int32, (1, 1, 8, width), 2)

    from_west = roll_columns(field, 1)
    from_east = roll_columns(field, -1)
    west = jnp.where(col == 0, shift_tiles(from_west, 1), from_west)
    east = jnp.where(col == width - 1, shift_tiles(from_east, -1), from_east)
    q = 0.5 * (field + jnp.where(col % 8 == 0, west, jnp.where(col % 8 == 7, east, field)))

    down = roll_nodes(q, 1)
    up = roll_nodes(q, -1)
    before = []
    after = []
    for first in range(0, blocks, elements):
        end = first + elements
        before += [q[:, first : first + 1], down[:, first : end - 1]]
        after += [up[:, first + 1 : end], q[:, end - 1 : end]]
    before = jnp.concatenate(before, axis=1)
    after = jnp.concatenate(after, axis=1)
    q = 0.5 * (q + jnp.where(node == 0, before, jnp.where(node == 7, after, q)))

    flux_x = (jnp.concatenate([wind_x, wind_x], axis=1) * q).reshape(-1, width)
    high, low = split_bf16(flux_x)
    grad_x = jnp.dot(
        jnp.concatenate([high, low], axis=1), along_x, preferred_element_type=jnp.float32
    )
    grad_x = (grad_x[:, :width] + grad_x[:, width:]).reshape(q.shape)

    flux_y = (jnp.concatenate([wind_y, wind_y], axis=1) * q).reshape(-1, 8, width)
    grad_y = along_y[0] * flux_y
    for shift in range(1, 8):
        grad_y = grad_y + along_y[shift] * pltpu.roll(flux_y, shift, 1)
    return q - (grad_x + grad_y.reshape(q.shape))


def sweep(own_ref, even_ref, odd_ref, far_refs, along_x_ref, along_y_ref, start, out_ref, last_moves):
    windows, _, rows, width = own_ref.shape
    found = places(windows)
    odd_place = lax.axis_index("space") % 2 == 1
    along_x = along_x_ref[...]
    along_y = [along_y_ref[shift] for shift in range(8)]
    col = lax.broadcasted_iota(jnp.int32, (rows, width), 1)
    col_tile = lax.broadcasted_iota(jnp.int32, (1, 1, 8, width), 3)

    def tiles(window, index, merged):
        tile, shift = found[(window, index)]
        by_even = even_ref[tile]
        by_odd = odd_ref[tile]
        for far_ref in far_refs:
            by_odd = by_odd + far_ref[tile]
        west = jnp.where(odd_place, by_even, by_odd)
        east = jnp.where(odd_place, by_odd, by_even)
        if shift:
            west = pltpu.roll(west, shift, 1)
            east = pltpu.roll(east, width - shift, 1)
        own = own_ref[window, index]
        if merged:
            parts = [own, jnp.where(col < width // 2, east, west)]
        else:
            parts = [own, east, west]
        return jnp.stack(parts).reshape(len(parts), rows // 8, 8, width)

    moved = start
    for window in range(windows - 1, -1, -1):
        merged = window < windows // 2
        field = jnp.concatenate([tiles(window, 4, merged), tiles(window, 5, merged)], axis=1)
        if moved is not None:
            if moved.shape[0] > field.shape[0]:
                side = jnp.where(col_tile < width // 2, moved[1:2], moved[2:3])
                moved = jnp.concatenate([moved[0:1], side], axis=0)
            field = field + moved
        here = field[0].reshape(2 * rows, width)
        out_ref[window, 0] = here[:rows]
        out_ref[window, 1] = here[rows:]
        if window == 0 and not last_moves:
            return None
        for substep in (1, 0):
            field = adjoint_step(
                field,
                tiles(window, substep, merged),
                tiles(window, 2 + substep, merged),
                along_x,
                along_y,
            )
        moved = field
    return moved[0].reshape(2 * rows, width)


def upper_kernel(
    own_ref, odd_ref, even_ref, to_odd_ref, along_x_ref, along_y_ref, out_ref, sent_ref, later_ref
):
    windows = own_ref.shape[0]

    @pl.when(lax.axis_index("tm") < windows)
    def _():
        later_ref[...] = to_odd_ref[...]

    @pl.when(lax.axis_index("tm") >= windows)
    def _():
        sent_ref[...] = sweep(
            own_ref, even_ref, odd_ref, (), along_x_ref, along_y_ref, None, out_ref, True
        )


def lower_kernel(
    done_ref, own_ref, even_ref, odd_ref, far_ref, along_x_ref, along_y_ref, here_ref, pe_ref, po_ref, out_ref
):
    windows, _, rows, width = own_ref.shape

    @pl.when(lax.axis_index("tm") < windows)
    def _():
        odd_place = lax.axis_index("space") % 2 == 1
        by_even = pe_ref[...]
        by_odd = po_ref[...]
        west = jnp.where(odd_place, by_even, by_odd)
        east = jnp.where(odd_place, by_odd, by_even)
        start = jnp.stack([here_ref[...], east, west]).reshape(3, 2 * rows // 8, 8, width)
        sweep(
            own_ref, even_ref, odd_ref, (far_ref,), along_x_ref, along_y_ref, start, out_ref, False
        )


def local_call(kernel, out_shape, in_specs, out_specs=None, vmem=32, **options):
    whole = pl.BlockSpec(memory_space=pltpu.VMEM)
    if isinstance(in_specs, int):
        in_specs = [whole] * in_specs
    return pl.pallas_call(
        kernel,
        out_shape=out_shape,
        in_specs=in_specs,
        out_specs=out_specs or jax.tree.map(lambda _: whole, out_shape),
        compiler_params=pltpu.CompilerParams(vmem_limit_bytes=vmem * 1024 * 1024),
        **options,
    )


def on_device(forcing, wind_x, wind_y):
    members, _, levels, rows, width = forcing.shape
    tm = lax.axis_size("tm")
    space = lax.axis_size("space")
    group = levels
    groups = [list(range(i, i + group)) for i in range(0, tm, group)]
    layer = space // 2
    anywhere = pl.BlockSpec(memory_space=pltpu.HBM)

    def same(t, s):
        return t, s

    def even_mate(t, s):
        return t, s ^ 1

    def is_far(s):
        return s % layer in (0, layer - 1)

    def odd_mate(t, s):
        mate = (s + 1) % space if s % 2 else (s - 1) % space
        return (t ^ (group // 2) if is_far(s) else t), mate

    def exchange(block, mate, chosen, dt=0):
        pairs = []
        for t in range(tm):
            for s in range(space):
                if chosen(t, s):
                    to_t, to_s = mate(t, s)
                    pairs.append((t * space + s, (to_t + dt) * space + to_s))
        return lax.ppermute(block, ("tm", "space"), pairs)

    def upper(t, s):
        return t >= group

    packed = local_call(
        gather_kernel,
        jax.ShapeDtypeStruct((levels, 6, rows, width), jnp.float32),
        [anywhere] * 3,
        vmem=61,
        scratch_shapes=[pltpu.SemaphoreType.DMA((12,))],
    )(wind_x, wind_y, forcing)
    own = lax.all_to_all(packed, "tm", 0, 0, axis_index_groups=groups, tiled=True)

    tiles = jax.ShapeDtypeStruct((len(pair_tiles(group)), rows, width), jnp.float32)
    to_even, to_odd = local_call(pack_kernel, (tiles, tiles), 1)(own)
    odd = exchange(to_odd, odd_mate, lambda t, s: upper(t, s) or not is_far(s))
    even = exchange(to_even, even_mate, lambda t, s: True)
    along_x, along_y = derivative_tables(width)
    result_shape = jax.ShapeDtypeStruct((group, members, rows, width), jnp.float32)
    flat_field = jax.ShapeDtypeStruct((members * rows, width), jnp.float32)
    done, sent, later = local_call(upper_kernel, (result_shape, flat_field, tiles), 6)(
        own, odd, even, to_odd, along_x, along_y
    )
    far = exchange(later, odd_mate, lambda t, s: is_far(s) and not upper(t, s))
    from_here = exchange(sent, same, upper, -group)
    from_even = exchange(sent, even_mate, upper, -group)
    from_odd = exchange(sent, odd_mate, upper, -group)
    result = local_call(lower_kernel, result_shape, 10, input_output_aliases={0: 0})(
        done, own, even, odd, far, along_x, along_y, from_here, from_even, from_odd
    )
    result = lax.all_to_all(result, "tm", 0, 0, axis_index_groups=groups, tiled=True)
    return local_call(
        scatter_kernel,
        jax.ShapeDtypeStruct(forcing.shape, jnp.float32),
        [pl.BlockSpec(memory_space=pltpu.VMEM)],
        anywhere,
        scratch_shapes=[pltpu.SemaphoreType.DMA((4,))],
    )(result)


def solution(mesh):
    placed = (
        P(None, "tm", None, None, "space"),
        P("tm", None, None, None, "space"),
        P("tm", None, None, None, "space"),
    )
    return jax.shard_map(
        on_device,
        mesh=mesh,
        in_specs=placed,
        out_specs=P(None, "tm", None, None, "space"),
        check_vma=False,
    )
```

```python
import functools

import jax
import jax.numpy as jnp
import numpy as np
from jax import lax
from jax.experimental import pallas as pl
from jax.experimental.pallas import tpu as pltpu
from jax.sharding import PartitionSpec as P

time_step = 0.01
lobatto_points = [
    -1.0,
    -0.8717401485096066,
    -0.5917001814331423,
    -0.20929921790247888,
    0.20929921790247888,
    0.5917001814331423,
    0.8717401485096066,
    1.0,
]


def legendre_seven(point):
    before = 1.0
    current = point
    for order in range(1, 7):
        before, current = (
            current,
            ((2 * order + 1) * point * current - order * before) / (order + 1),
        )
    return current


def lobatto_table():
    values = [legendre_seven(point) for point in lobatto_points]
    table = np.zeros((8, 8))
    for row_index in range(8):
        for col_index in range(8):
            if row_index != col_index:
                table[row_index, col_index] = values[row_index] / (
                    values[col_index] * (lobatto_points[row_index] - lobatto_points[col_index])
                )
    table[0, 0] = -14.0
    table[7, 7] = 14.0
    return table.astype(np.float32)


def split_bf16(value):
    high = value.astype(jnp.bfloat16)
    return high, (value - high.astype(jnp.float32)).astype(jnp.bfloat16)


def derivative_tables(width):
    table = lobatto_table() * np.float32(time_step)
    along_x = np.kron(np.eye(width // 8, dtype=np.float32), table)
    high = along_x.astype(jnp.bfloat16)
    low = (along_x - high.astype(np.float32)).astype(jnp.bfloat16)
    product = np.zeros((2 * width, 2 * width), jnp.bfloat16)
    product[:width, :width] = high
    product[width:, :width] = high
    product[:width, width:] = low
    along_y = np.zeros((8, 8, width), np.float32)
    for shift in range(8):
        for node in range(8):
            along_y[shift, node, :] = table[(node - shift) % 8, node]
    return jnp.asarray(product), jnp.asarray(along_y)


def pair_tiles(windows):
    last = 2 * windows
    tiles = []

    def block(step, kind):
        return (windows - 1 - (step - 1) // 2, 2 * kind + (step % 2))

    for step in range(1, windows + 1):
        for kind in (0, 1):
            tiles.append((block(step, kind), block(last + 1 - step, kind), 8 * (last - step)))
    tiles.append(((windows - 1, 4), None, 16 * windows))
    tiles.append(((windows - 1, 5), None, 16 * windows))
    for window in range(windows - 2, windows // 2 - 1, -1):
        for member in (4, 5):
            tiles.append(
                ((window, member), (windows - 2 - window, member), 16 * (window + 1))
            )
    middle = windows // 2 - 1
    tiles.append(((middle, 4), (middle, 5), 16 * (middle + 1)))
    return tiles


def places(windows):
    found = {}
    for index, (first, second, columns) in enumerate(pair_tiles(windows)):
        found[first] = (index, 0)
        if second is not None:
            found[second] = (index, columns)
    return found


def layer_here():
    return lax.axis_index("space") // (lax.axis_size("space") // 2)


def gather_kernel(wind_x_ref, wind_y_ref, forcing_ref, out_ref, sems):
    levels = out_ref.shape[0]
    half = levels // 2
    layer = layer_here()
    copies = []
    for part in (0, 1):
        here = pl.ds(half * part, half)
        there = pl.ds(half * jnp.bitwise_xor(layer, part), half)
        for index in (0, 1):
            copies.append((wind_x_ref.at[0, index, here], out_ref.at[there, index]))
            copies.append((wind_y_ref.at[0, index, here], out_ref.at[there, 2 + index]))
            copies.append((forcing_ref.at[index, 0, here], out_ref.at[there, 4 + index]))
    copies = [
        pltpu.make_async_copy(source, target, sems.at[index])
        for index, (source, target) in enumerate(copies)
    ]
    for copy in copies:
        copy.start()
    for copy in copies:
        copy.wait()


def scatter_kernel(in_ref, out_ref, sems):
    levels = in_ref.shape[0]
    half = levels // 2
    layer = layer_here()
    copies = []
    for part in (0, 1):
        here = pl.ds(half * part, half)
        there = pl.ds(half * jnp.bitwise_xor(layer, part), half)
        for member in (0, 1):
            copies.append(
                pltpu.make_async_copy(
                    in_ref.at[there, member],
                    out_ref.at[member, 0, here],
                    sems.at[2 * part + member],
                )
            )
    for copy in copies:
        copy.start()
    for copy in copies:
        copy.wait()


def pack_kernel(towards_even, own_ref, *refs):
    out_ref = refs[-1]
    windows, _, rows, width = own_ref.shape
    col = lax.broadcasted_iota(jnp.int32, (rows, width), 1)
    to_east = (lax.axis_index("space") % 2 == 0) == towards_even

    def write(high):
        for index, (first, second, columns) in enumerate(pair_tiles(windows)):
            value = own_ref[first[0], first[1]]
            if second is not None:
                other = own_ref[second[0], second[1]]
                if high:
                    keep = col >= width - columns
                    other = pltpu.roll(other, width - columns, 1)
                else:
                    keep = col < columns
                    other = pltpu.roll(other, columns, 1)
                value = jnp.where(keep, value, other)
            out_ref[index] = value

    @pl.when(to_east)
    def _():
        write(True)

    @pl.when(jnp.logical_not(to_east))
    def _():
        write(False)


def shift_tiles(tiles, distance):
    distance %= tiles.shape[0]
    return jnp.concatenate([tiles[-distance:], tiles[:-distance]], axis=0)


def roll_columns(value, distance):
    width = value.shape[-1]
    return pltpu.roll(value.reshape(-1, width), distance % width, 1).reshape(value.shape)


def roll_nodes(value, distance):
    width = value.shape[-1]
    return pltpu.roll(value.reshape(-1, 8, width), distance % 8, 1).reshape(value.shape)


def adjoint_step(field, wind_x, wind_y, along_x, along_y):
    count, blocks, _, width = field.shape
    elements = blocks // 2
    col = lax.broadcasted_iota(jnp.int32, (1, 1, 8, width), 3)
    node = lax.broadcasted_iota(jnp.int32, (1, 1, 8, width), 2)

    from_west = roll_columns(field, 1)
    from_east = roll_columns(field, -1)
    west = jnp.where(col == 0, shift_tiles(from_west, 1), from_west)
    east = jnp.where(col == width - 1, shift_tiles(from_east, -1), from_east)
    q = 0.5 * (field + jnp.where(col % 8 == 0, west, jnp.where(col % 8 == 7, east, field)))

    down = roll_nodes(q, 1)
    up = roll_nodes(q, -1)
    before = []
    after = []
    for first in range(0, blocks, elements):
        end = first + elements
        before += [q[:, first : first + 1], down[:, first : end - 1]]
        after += [up[:, first + 1 : end], q[:, end - 1 : end]]
    before = jnp.concatenate(before, axis=1)
    after = jnp.concatenate(after, axis=1)
    q = 0.5 * (q + jnp.where(node == 0, before, jnp.where(node == 7, after, q)))

    flux_x = (jnp.concatenate([wind_x, wind_x], axis=1) * q).reshape(-1, width)
    high, low = split_bf16(flux_x)
    grad_x = jnp.dot(
        jnp.concatenate([high, low], axis=1), along_x, preferred_element_type=jnp.float32
    )
    grad_x = (grad_x[:, :width] + grad_x[:, width:]).reshape(q.shape)

    flux_y = (jnp.concatenate([wind_y, wind_y], axis=1) * q).reshape(-1, 8, width)
    grad_y = along_y[0] * flux_y
    for shift in range(1, 8):
        grad_y = grad_y + along_y[shift] * pltpu.roll(flux_y, shift, 1)
    return q - (grad_x + grad_y.reshape(q.shape))


def sweep(own_ref, even_ref, odd_ref, far_refs, along_x_ref, along_y_ref, start, out_ref, last_moves):
    windows, _, rows, width = own_ref.shape
    found = places(windows)
    odd_place = lax.axis_index("space") % 2 == 1
    along_x = along_x_ref[...]
    along_y = [along_y_ref[shift] for shift in range(8)]
    col = lax.broadcasted_iota(jnp.int32, (rows, width), 1)
    col_tile = lax.broadcasted_iota(jnp.int32, (1, 1, 8, width), 3)

    def tiles(window, index, merged):
        tile, shift = found[(window, index)]
        by_even = even_ref[tile]
        by_odd = odd_ref[tile]
        for far_ref in far_refs:
            by_odd = by_odd + far_ref[tile]
        west = jnp.where(odd_place, by_even, by_odd)
        east = jnp.where(odd_place, by_odd, by_even)
        if shift:
            west = pltpu.roll(west, shift, 1)
            east = pltpu.roll(east, width - shift, 1)
        own = own_ref[window, index]
        if merged:
            parts = [own, jnp.where(col < width // 2, east, west)]
        else:
            parts = [own, east, west]
        return jnp.stack(parts).reshape(len(parts), rows // 8, 8, width)

    moved = start
    for window in range(windows - 1, -1, -1):
        merged = window < windows // 2
        field = jnp.concatenate([tiles(window, 4, merged), tiles(window, 5, merged)], axis=1)
        if moved is not None:
            if moved.shape[0] > field.shape[0]:
                side = jnp.where(col_tile < width // 2, moved[1:2], moved[2:3])
                moved = jnp.concatenate([moved[0:1], side], axis=0)
            field = field + moved
        here = field[0].reshape(2 * rows, width)
        out_ref[window, 0] = here[:rows]
        out_ref[window, 1] = here[rows:]
        if window == 0 and not last_moves:
            return None
        for substep in (1, 0):
            field = adjoint_step(
                field,
                tiles(window, substep, merged),
                tiles(window, 2 + substep, merged),
                along_x,
                along_y,
            )
        moved = field
    return moved[0].reshape(2 * rows, width)


def upper_kernel(own_ref, odd_ref, even_ref, along_x_ref, along_y_ref, out_ref, sent_ref):
    windows = own_ref.shape[0]

    @pl.when(lax.axis_index("tm") >= windows)
    def _():
        sent_ref[...] = sweep(
            own_ref, even_ref, odd_ref, (), along_x_ref, along_y_ref, None, out_ref, True
        )


def lower_kernel(
    done_ref, own_ref, even_ref, odd_ref, far_ref, along_x_ref, along_y_ref, here_ref, pe_ref, po_ref, out_ref
):
    windows, _, rows, width = own_ref.shape

    @pl.when(lax.axis_index("tm") < windows)
    def _():
        odd_place = lax.axis_index("space") % 2 == 1
        by_even = pe_ref[...]
        by_odd = po_ref[...]
        west = jnp.where(odd_place, by_even, by_odd)
        east = jnp.where(odd_place, by_odd, by_even)
        start = jnp.stack([here_ref[...], east, west]).reshape(3, 2 * rows // 8, 8, width)
        sweep(
            own_ref, even_ref, odd_ref, (far_ref,), along_x_ref, along_y_ref, start, out_ref, False
        )


def local_call(kernel, out_shape, in_specs, out_specs=None, vmem=32, **options):
    whole = pl.BlockSpec(memory_space=pltpu.VMEM)
    if isinstance(in_specs, int):
        in_specs = [whole] * in_specs
    return pl.pallas_call(
        kernel,
        out_shape=out_shape,
        in_specs=in_specs,
        out_specs=out_specs or jax.tree.map(lambda _: whole, out_shape),
        compiler_params=pltpu.CompilerParams(vmem_limit_bytes=vmem * 1024 * 1024),
        **options,
    )


def on_device(forcing, wind_x, wind_y):
    members, _, levels, rows, width = forcing.shape
    tm = lax.axis_size("tm")
    space = lax.axis_size("space")
    group = levels
    groups = [list(range(i, i + group)) for i in range(0, tm, group)]
    layer = space // 2
    anything = pl.BlockSpec(memory_space=pl.ANY)
    anywhere = pl.BlockSpec(memory_space=pltpu.HBM)

    def same(t, s):
        return t, s

    def even_mate(t, s):
        return t, s ^ 1

    def is_far(s):
        return s % layer in (0, layer - 1)

    def odd_mate(t, s):
        mate = (s + 1) % space if s % 2 else (s - 1) % space
        return (t ^ (group // 2) if is_far(s) else t), mate

    def exchange(block, mate, chosen, dt=0):
        pairs = []
        for t in range(tm):
            for s in range(space):
                if chosen(t, s):
                    to_t, to_s = mate(t, s)
                    pairs.append((t * space + s, (to_t + dt) * space + to_s))
        return lax.ppermute(block, ("tm", "space"), pairs)

    def upper(t, s):
        return t >= group

    packed = local_call(
        gather_kernel,
        jax.ShapeDtypeStruct((levels, 6, rows, width), jnp.float32),
        [anywhere] * 3,
        vmem=61,
        scratch_shapes=[pltpu.SemaphoreType.DMA((12,))],
    )(wind_x, wind_y, forcing)
    own = lax.all_to_all(packed, "tm", 0, 0, axis_index_groups=groups, tiled=True)

    tiles = jax.ShapeDtypeStruct((len(pair_tiles(group)), rows, width), jnp.float32)
    to_odd = local_call(functools.partial(pack_kernel, False), tiles, 1)(own)
    odd = exchange(to_odd, odd_mate, lambda t, s: upper(t, s) or not is_far(s))
    relayed = exchange(to_odd, even_mate, lambda t, s: is_far(s) and not upper(t, s))
    far = exchange(
        relayed, lambda t, s: odd_mate(t, s ^ 1), lambda t, s: is_far(s ^ 1) and not upper(t, s)
    )
    to_even = local_call(
        functools.partial(pack_kernel, True), tiles, [pl.BlockSpec(memory_space=pltpu.VMEM), anything]
    )(own, relayed)
    even = exchange(to_even, even_mate, lambda t, s: True)
    along_x, along_y = derivative_tables(width)
    result_shape = jax.ShapeDtypeStruct((group, members, rows, width), jnp.float32)
    flat_field = jax.ShapeDtypeStruct((members * rows, width), jnp.float32)
    done, sent = local_call(upper_kernel, (result_shape, flat_field), 5)(
        own, odd, even, along_x, along_y
    )
    from_here = exchange(sent, same, upper, -group)
    from_even = exchange(sent, even_mate, upper, -group)
    from_odd = exchange(sent, odd_mate, upper, -group)
    result = local_call(lower_kernel, result_shape, 10, input_output_aliases={0: 0})(
        done, own, even, odd, far, along_x, along_y, from_here, from_even, from_odd
    )
    result = lax.all_to_all(result, "tm", 0, 0, axis_index_groups=groups, tiled=True)
    return local_call(
        scatter_kernel,
        jax.ShapeDtypeStruct(forcing.shape, jnp.float32),
        [pl.BlockSpec(memory_space=pltpu.VMEM)],
        anywhere,
        scratch_shapes=[pltpu.SemaphoreType.DMA((4,))],
    )(result)


def solution(mesh):
    placed = (
        P(None, "tm", None, None, "space"),
        P("tm", None, None, None, "space"),
        P("tm", None, None, None, "space"),
    )
    return jax.shard_map(
        on_device,
        mesh=mesh,
        in_specs=placed,
        out_specs=P(None, "tm", None, None, "space"),
        check_vma=False,
    )
```

```python
import jax
import jax.numpy as jnp
import numpy as np
from jax import lax
from jax.experimental import pallas as pl
from jax.experimental.pallas import tpu as pltpu
from jax.sharding import PartitionSpec as P

time_step = 0.01
lobatto_points = [
    -1.0,
    -0.8717401485096066,
    -0.5917001814331423,
    -0.20929921790247888,
    0.20929921790247888,
    0.5917001814331423,
    0.8717401485096066,
    1.0,
]


def legendre_seven(point):
    before = 1.0
    current = point
    for order in range(1, 7):
        before, current = (
            current,
            ((2 * order + 1) * point * current - order * before) / (order + 1),
        )
    return current


def lobatto_table():
    values = [legendre_seven(point) for point in lobatto_points]
    table = np.zeros((8, 8))
    for row_index in range(8):
        for col_index in range(8):
            if row_index != col_index:
                table[row_index, col_index] = values[row_index] / (
                    values[col_index] * (lobatto_points[row_index] - lobatto_points[col_index])
                )
    table[0, 0] = -14.0
    table[7, 7] = 14.0
    return table.astype(np.float32)


def split_bf16(value):
    high = value.astype(jnp.bfloat16)
    return high, (value - high.astype(jnp.float32)).astype(jnp.bfloat16)


def derivative_tables(width):
    table = lobatto_table() * np.float32(time_step)
    along_x = np.kron(np.eye(width // 8, dtype=np.float32), table)
    high = along_x.astype(jnp.bfloat16)
    low = (along_x - high.astype(np.float32)).astype(jnp.bfloat16)
    product = np.zeros((2 * width, 2 * width), jnp.bfloat16)
    product[:width, :width] = high
    product[width:, :width] = high
    product[:width, width:] = low
    along_y = np.zeros((8, 8, width), np.float32)
    for shift in range(8):
        for node in range(8):
            along_y[shift, node, :] = table[(node - shift) % 8, node]
    return jnp.asarray(product), jnp.asarray(along_y)


def triangle_tiles(windows):
    last = 2 * windows
    width = 8 * last
    tiles = []
    for step in range(1, windows + 1):
        for kind in (0, 1):
            cut = 8 * (last - step)
            tiles.append(
                [
                    (block_of(windows, step, kind), 0, cut),
                    (block_of(windows, last + 1 - step, kind), cut, width - cut),
                ]
            )
    tiles.append([((windows - 1, 4), 0, width)])
    tiles.append([((windows - 1, 5), 0, width)])
    for window in range(windows - 2, windows // 2 - 1, -1):
        for member in (4, 5):
            cut = 16 * (window + 1)
            tiles.append(
                [((window, member), 0, cut), ((windows - 2 - window, member), cut, width - cut)]
            )
    middle = windows // 2 - 1
    cut = 16 * (middle + 1)
    tiles.append([((middle, 4), 0, cut), ((middle, 5), cut, width - cut)])
    return tiles


def block_of(windows, step, kind):
    return (windows - 1 - (step - 1) // 2, 2 * kind + (step % 2))


def diamond_tiles(windows):
    last = 2 * windows
    tiles = []

    def fill(blocks):
        offset = 0
        tile = []
        for block, elements in blocks:
            tile.append((block, offset, 8 * elements))
            offset += 8 * elements
        tiles.append(tile)

    for kind in (0, 1):
        for step in range(1, windows // 2):
            group = (step, windows - step, last - step, windows + step)
            fill([(block_of(windows, n, kind), min(n, last - n)) for n in group])
        group = (windows // 2, last - windows // 2, windows)
        fill([(block_of(windows, n, kind), min(n, last - n)) for n in group])

    def forcing_elements(window):
        step = 2 * (windows - 1 - window) + 1
        return min(step - 1, last + 1 - step)

    for member in (4, 5):
        for group in ((6, 4, 3), (5, 2, 1, 0)):
            fill([((window, member), forcing_elements(window)) for window in group])
    return tiles


def places(tiles):
    found = {}
    for index, tile in enumerate(tiles):
        for block, offset, _ in tile:
            found[block] = (index, offset)
    return found


def layer_here():
    return lax.axis_index("space") // (lax.axis_size("space") // 2)


def gather_kernel(wind_x_ref, wind_y_ref, forcing_ref, out_ref, sems):
    levels = out_ref.shape[0]
    half = levels // 2
    layer = layer_here()
    copies = []
    for part in (0, 1):
        here = pl.ds(half * part, half)
        there = pl.ds(half * jnp.bitwise_xor(layer, part), half)
        for index in (0, 1):
            copies.append((wind_x_ref.at[0, index, here], out_ref.at[there, index]))
            copies.append((wind_y_ref.at[0, index, here], out_ref.at[there, 2 + index]))
            copies.append((forcing_ref.at[index, 0, here], out_ref.at[there, 4 + index]))
    copies = [
        pltpu.make_async_copy(source, target, sems.at[index])
        for index, (source, target) in enumerate(copies)
    ]
    for copy in copies:
        copy.start()
    for copy in copies:
        copy.wait()


def scatter_kernel(in_ref, out_ref, sems):
    levels = in_ref.shape[0]
    half = levels // 2
    layer = layer_here()
    copies = []
    for part in (0, 1):
        here = pl.ds(half * part, half)
        there = pl.ds(half * jnp.bitwise_xor(layer, part), half)
        for member in (0, 1):
            copies.append(
                pltpu.make_async_copy(
                    in_ref.at[there, member],
                    out_ref.at[member, 0, here],
                    sems.at[2 * part + member],
                )
            )
    for copy in copies:
        copy.start()
    for copy in copies:
        copy.wait()


def columns_at(col, offset, columns, high):
    width = col.shape[-1]
    if high:
        offset = width - offset - columns
    return (col >= offset) & (col < offset + columns)


def pack_tiles(own_ref, layout, high, out_ref):
    width = own_ref.shape[3]
    col = lax.broadcasted_iota(jnp.int32, own_ref.shape[2:], 1)
    for index, tile in enumerate(layout):
        value = None
        for block, offset, columns in tile:
            one = own_ref[block[0], block[1]]
            if offset:
                one = pltpu.roll(one, width - offset if high else offset, 1)
            if value is None:
                value = one
            else:
                value = jnp.where(columns_at(col, offset, columns, high), one, value)
        out_ref[index] = value


def pack_sides(layout, own_ref, even_ref, odd_ref):
    odd_place = lax.axis_index("space") % 2 == 1

    @pl.when(odd_place)
    def _():
        pack_tiles(own_ref, layout, False, even_ref)
        pack_tiles(own_ref, layout, True, odd_ref)

    @pl.when(jnp.logical_not(odd_place))
    def _():
        pack_tiles(own_ref, layout, True, even_ref)
        pack_tiles(own_ref, layout, False, odd_ref)


def pack_relay_kernel(own_ref, first_ref, second_ref):
    windows = own_ref.shape[0]
    cut = first_ref.shape[0]
    odd_place = lax.axis_index("space") % 2 == 1
    in_lower = lax.axis_index("tm") < windows

    def pack(high):
        layout = triangle_tiles(windows)
        pack_tiles(own_ref, layout[:cut], high, first_ref)
        pack_tiles(own_ref, layout[cut:], high, second_ref)

    @pl.when(jnp.logical_and(in_lower, odd_place))
    def _():
        pack(True)

    @pl.when(jnp.logical_and(in_lower, jnp.logical_not(odd_place)))
    def _():
        pack(False)


def pack_lower_kernel(own_ref, b1_ref, b2_ref, b3_ref, b4_ref, even_ref, odd_ref):
    windows = own_ref.shape[0]

    @pl.when(lax.axis_index("tm") < windows)
    def _():
        pack_sides(triangle_tiles(windows), own_ref, even_ref, odd_ref)


def pack_upper_kernel(own_ref, along_x_ref, along_y_ref, even_ref, odd_ref):
    windows, _, rows, width = own_ref.shape
    odd_place = lax.axis_index("space") % 2 == 1

    @pl.when(lax.axis_index("tm") >= windows)
    def _():
        layout = diamond_tiles(windows)
        pack_sides(layout, own_ref, even_ref, odd_ref)
        along_x = along_x_ref[...]
        along_y = [along_y_ref[shift] for shift in range(8)]
        col = lax.broadcasted_iota(jnp.int32, (2 * rows, width), 1)

        def tile(window, index):
            return own_ref[window, index].reshape(1, rows // 8, 8, width)

        field = None
        low = high = None
        for step in range(1, windows + 1):
            window = windows - 1 - (step - 1) // 2
            if step % 2:
                forcing = jnp.concatenate([tile(window, 4), tile(window, 5)], axis=1)
                field = forcing if field is None else field + forcing
            here = field.reshape(2 * rows, width)
            if step == 1:
                low = high = here
            else:
                shift = 8 * (step - 1)
                wanted = columns_at(col, 2 * shift, 16, False)
                low = jnp.where(wanted, pltpu.roll(here, shift, 1), low)
                wanted = columns_at(col, 2 * shift, 16, True)
                high = jnp.where(wanted, pltpu.roll(here, width - shift, 1), high)
            if step < windows:
                field = adjoint_step(
                    field, tile(window, step % 2), tile(window, 2 + step % 2), along_x, along_y
                )
        first = len(layout)
        to_even = jnp.where(odd_place, low, high)
        to_odd = jnp.where(odd_place, high, low)
        even_ref[first] = to_even[:rows]
        even_ref[first + 1] = to_even[rows:]
        odd_ref[first] = to_odd[:rows]
        odd_ref[first + 1] = to_odd[rows:]


def shift_tiles(tiles, distance):
    distance %= tiles.shape[0]
    if distance == 0:
        return tiles
    return jnp.concatenate([tiles[-distance:], tiles[:-distance]], axis=0)


def roll_columns(value, distance):
    width = value.shape[-1]
    return pltpu.roll(value.reshape(-1, width), distance % width, 1).reshape(value.shape)


def roll_nodes(value, distance):
    width = value.shape[-1]
    return pltpu.roll(value.reshape(-1, 8, width), distance % 8, 1).reshape(value.shape)


def adjoint_step(field, wind_x, wind_y, along_x, along_y):
    count, blocks, _, width = field.shape
    elements = blocks // 2
    col = lax.broadcasted_iota(jnp.int32, (1, 1, 8, width), 3)
    node = lax.broadcasted_iota(jnp.int32, (1, 1, 8, width), 2)

    from_west = roll_columns(field, 1)
    from_east = roll_columns(field, -1)
    west = jnp.where(col == 0, shift_tiles(from_west, 1), from_west)
    east = jnp.where(col == width - 1, shift_tiles(from_east, -1), from_east)
    q = 0.5 * (field + jnp.where(col % 8 == 0, west, jnp.where(col % 8 == 7, east, field)))

    down = roll_nodes(q, 1)
    up = roll_nodes(q, -1)
    before = []
    after = []
    for first in range(0, blocks, elements):
        end = first + elements
        before += [q[:, first : first + 1], down[:, first : end - 1]]
        after += [up[:, first + 1 : end], q[:, end - 1 : end]]
    before = jnp.concatenate(before, axis=1)
    after = jnp.concatenate(after, axis=1)
    q = 0.5 * (q + jnp.where(node == 0, before, jnp.where(node == 7, after, q)))

    flux_x = (jnp.concatenate([wind_x, wind_x], axis=1) * q).reshape(-1, width)
    high, low = split_bf16(flux_x)
    grad_x = jnp.dot(
        jnp.concatenate([high, low], axis=1), along_x, preferred_element_type=jnp.float32
    )
    grad_x = (grad_x[:, :width] + grad_x[:, width:]).reshape(q.shape)

    flux_y = (jnp.concatenate([wind_y, wind_y], axis=1) * q).reshape(-1, 8, width)
    grad_y = along_y[0] * flux_y
    for shift in range(1, 8):
        grad_y = grad_y + along_y[shift] * pltpu.roll(flux_y, shift, 1)
    return q - (grad_x + grad_y.reshape(q.shape))


def sweep(
    own_ref, even_ref, odd_ref, far_refs, along_x_ref, along_y_ref, start, out_ref, upper
):
    windows, _, rows, width = own_ref.shape
    layout = diamond_tiles(windows) if upper else triangle_tiles(windows)
    found = places(layout)
    odd_place = lax.axis_index("space") % 2 == 1
    along_x = along_x_ref[...]
    along_y = [along_y_ref[shift] for shift in range(8)]
    col = lax.broadcasted_iota(jnp.int32, (rows, width), 1)
    col_tile = lax.broadcasted_iota(jnp.int32, (1, 1, 8, width), 3)

    def sides(tile, shift):
        by_even = even_ref[tile]
        by_odd = odd_ref[tile]
        first = 0
        for far_ref in far_refs:
            if first <= tile < first + far_ref.shape[0]:
                by_odd = by_odd + far_ref[tile - first]
            first += far_ref.shape[0]
        west = jnp.where(odd_place, by_even, by_odd)
        east = jnp.where(odd_place, by_odd, by_even)
        if shift:
            west = pltpu.roll(west, shift, 1)
            east = pltpu.roll(east, width - shift, 1)
        return east, west

    def tiles(window, index, merged):
        own = own_ref[window, index]
        if (window, index) in found:
            east, west = sides(*found[(window, index)])
        else:
            east = west = jnp.zeros_like(own)
        if merged:
            parts = [own, jnp.where(col < width // 2, east, west)]
        else:
            parts = [own, east, west]
        return jnp.stack(parts).reshape(len(parts), rows // 8, 8, width)

    def with_finished(field, step):
        shift = 8 * (step - 1)
        pairs = [sides(len(layout) + member, shift) for member in (0, 1)]
        east = jnp.stack([pair[0] for pair in pairs]).reshape(1, 2 * rows // 8, 8, width)
        west = jnp.stack([pair[1] for pair in pairs]).reshape(1, 2 * rows // 8, 8, width)
        east = jnp.where(columns_at(col_tile, shift, 16, False), east, field[1:2])
        west = jnp.where(columns_at(col_tile, shift, 16, True), west, field[2:3])
        return jnp.concatenate([field[0:1], east, west], axis=0)

    moved = start
    for window in range(windows - 1, -1, -1):
        merged = window < windows // 2
        field = jnp.concatenate([tiles(window, 4, merged), tiles(window, 5, merged)], axis=1)
        if moved is not None:
            if moved.shape[0] > field.shape[0]:
                side = jnp.where(col_tile < width // 2, moved[1:2], moved[2:3])
                moved = jnp.concatenate([moved[0:1], side], axis=0)
            field = field + moved
        here = field[0].reshape(2 * rows, width)
        out_ref[window, 0] = here[:rows]
        out_ref[window, 1] = here[rows:]
        if window == 0 and not upper:
            return None
        for substep in (1, 0):
            step = 2 * (windows - window) - substep
            if upper and step <= windows:
                field = with_finished(field, step)
            field = adjoint_step(
                field,
                tiles(window, substep, merged),
                tiles(window, 2 + substep, merged),
                along_x,
                along_y,
            )
        moved = field
    return moved[0].reshape(2 * rows, width)


def upper_kernel(
    own_ref,
    odd_ref,
    even_ref,
    b1_ref,
    b2_ref,
    along_x_ref,
    along_y_ref,
    out_ref,
    sent_ref,
):
    windows = own_ref.shape[0]

    @pl.when(lax.axis_index("tm") >= windows)
    def _():
        sent_ref[...] = sweep(
            own_ref, even_ref, odd_ref, (), along_x_ref, along_y_ref, None, out_ref, True
        )


def lower_kernel(
    done_ref,
    own_ref,
    even_ref,
    odd_ref,
    far_x_ref,
    far_y_ref,
    along_x_ref,
    along_y_ref,
    here_ref,
    pe_ref,
    po_ref,
    out_ref,
):
    windows, _, rows, width = own_ref.shape

    @pl.when(lax.axis_index("tm") < windows)
    def _():
        odd_place = lax.axis_index("space") % 2 == 1
        by_even = pe_ref[...]
        by_odd = po_ref[...]
        west = jnp.where(odd_place, by_even, by_odd)
        east = jnp.where(odd_place, by_odd, by_even)
        far_refs = (far_x_ref, far_y_ref)
        start = jnp.stack([here_ref[...], east, west]).reshape(3, 2 * rows // 8, 8, width)
        sweep(
            own_ref, even_ref, odd_ref, far_refs, along_x_ref, along_y_ref, start, out_ref, False
        )


def local_call(kernel, out_shape, in_specs, out_specs=None, vmem=32, **options):
    whole = pl.BlockSpec(memory_space=pltpu.VMEM)
    if isinstance(in_specs, int):
        in_specs = [whole] * in_specs
    return pl.pallas_call(
        kernel,
        out_shape=out_shape,
        in_specs=in_specs,
        out_specs=out_specs or jax.tree.map(lambda _: whole, out_shape),
        compiler_params=pltpu.CompilerParams(vmem_limit_bytes=vmem * 1024 * 1024),
        **options,
    )


def on_device(forcing, wind_x, wind_y):
    members, _, levels, rows, width = forcing.shape
    tm = lax.axis_size("tm")
    space = lax.axis_size("space")
    group = levels
    groups = [list(range(i, i + group)) for i in range(0, tm, group)]
    layer = space // 2
    anything = pl.BlockSpec(memory_space=pl.ANY)
    anywhere = pl.BlockSpec(memory_space=pltpu.HBM)

    def same(t, s):
        return t, s

    def even_mate(t, s):
        return t, s ^ 1

    def is_far(s):
        return s % layer in (0, layer - 1)

    def odd_mate(t, s):
        mate = (s + 1) % space if s % 2 else (s - 1) % space
        return (t ^ (group // 2) if is_far(s) else t), mate

    def along_y_mate(t, s):
        row = max(2, layer // 4)
        return t, (s + row if s % layer == 0 else s - row)

    def exchange(block, mate, chosen, dt=0):
        pairs = []
        for t in range(tm):
            for s in range(space):
                if chosen(t, s):
                    to_t, to_s = mate(t, s)
                    pairs.append((t * space + s, (to_t + dt) * space + to_s))
        return lax.ppermute(block, ("tm", "space"), pairs)

    def upper(t, s):
        return t >= group

    packed = local_call(
        gather_kernel,
        jax.ShapeDtypeStruct((levels, 6, rows, width), jnp.float32),
        [anywhere] * 3,
        vmem=61,
        scratch_shapes=[pltpu.SemaphoreType.DMA((12,))],
    )(wind_x, wind_y, forcing)
    own = lax.all_to_all(packed, "tm", 0, 0, axis_index_groups=groups, tiled=True)

    whole = pl.BlockSpec(memory_space=pltpu.VMEM)
    anything = pl.BlockSpec(memory_space=pl.ANY)
    along_x, along_y = derivative_tables(width)

    def tiles(number):
        return jax.ShapeDtypeStruct((number, rows, width), jnp.float32)

    def lower(t, s):
        return not upper(t, s)

    diamond = tiles(len(diamond_tiles(group)) + 2)
    triangle = tiles(len(triangle_tiles(group)))
    to_even, to_odd = local_call(pack_upper_kernel, (diamond, diamond), 3)(own, along_x, along_y)
    upper_odd = exchange(to_odd, odd_mate, upper)
    upper_even = exchange(to_even, even_mate, upper)

    cut = (len(triangle_tiles(group)) + 1) // 2
    halves = tiles(cut), tiles(len(triangle_tiles(group)) - cut)
    first_half, second_half = local_call(pack_relay_kernel, halves, 1)(own)

    def relay(block, neighbour):
        there = exchange(block, neighbour, lambda t, s: is_far(s) and lower(t, s))
        pairs = []
        for t in range(group):
            for s in range(space):
                if is_far(s):
                    from_t, from_s = neighbour(t, s)
                    to_t, to_s = odd_mate(t, s)
                    pairs.append((from_t * space + from_s, to_t * space + to_s))
        return there, lax.ppermute(there, ("tm", "space"), pairs)

    there_x, far_x = relay(first_half, even_mate)
    there_y, far_y = relay(second_half, along_y_mate)
    to_even, to_odd = local_call(
        pack_lower_kernel, (triangle, triangle), [whole] + [anything] * 4
    )(own, upper_odd, upper_even, there_x, there_y)
    lower_odd = exchange(to_odd, odd_mate, lambda t, s: lower(t, s) and not is_far(s))
    lower_even = exchange(to_even, even_mate, lower)

    result_shape = jax.ShapeDtypeStruct((group, members, rows, width), jnp.float32)
    flat_field = jax.ShapeDtypeStruct((members * rows, width), jnp.float32)
    done, sent = local_call(
        upper_kernel,
        (result_shape, flat_field),
        [whole] * 3 + [anything] * 2 + [whole] * 2,
    )(own, upper_odd, upper_even, lower_odd, lower_even, along_x, along_y)
    from_here = exchange(sent, same, upper, -group)
    from_even = exchange(sent, even_mate, upper, -group)
    from_odd = exchange(sent, odd_mate, upper, -group)
    result = local_call(lower_kernel, result_shape, 11, input_output_aliases={0: 0})(
        done, own, lower_even, lower_odd, far_x, far_y, along_x, along_y, from_here, from_even, from_odd
    )
    result = lax.all_to_all(result, "tm", 0, 0, axis_index_groups=groups, tiled=True)
    return local_call(
        scatter_kernel,
        jax.ShapeDtypeStruct(forcing.shape, jnp.float32),
        [pl.BlockSpec(memory_space=pltpu.VMEM)],
        anywhere,
        scratch_shapes=[pltpu.SemaphoreType.DMA((4,))],
    )(result)


def solution(mesh):
    placed = (
        P(None, "tm", None, None, "space"),
        P("tm", None, None, None, "space"),
        P("tm", None, None, None, "space"),
    )
    return jax.shard_map(
        on_device,
        mesh=mesh,
        in_specs=placed,
        out_specs=P(None, "tm", None, None, "space"),
        check_vma=False,
    )
```

```python
import jax
import jax.numpy as jnp
import numpy as np
from jax import lax
from jax.experimental import pallas as pl
from jax.experimental.pallas import tpu as pltpu
from jax.sharding import PartitionSpec as P

time_step = 0.01
lobatto_points = [
    -1.0,
    -0.8717401485096066,
    -0.5917001814331423,
    -0.20929921790247888,
    0.20929921790247888,
    0.5917001814331423,
    0.8717401485096066,
    1.0,
]


def legendre_seven(point):
    before = 1.0
    current = point
    for order in range(1, 7):
        before, current = (
            current,
            ((2 * order + 1) * point * current - order * before) / (order + 1),
        )
    return current


def lobatto_table():
    values = [legendre_seven(point) for point in lobatto_points]
    table = np.zeros((8, 8))
    for row_index in range(8):
        for col_index in range(8):
            if row_index != col_index:
                table[row_index, col_index] = values[row_index] / (
                    values[col_index] * (lobatto_points[row_index] - lobatto_points[col_index])
                )
    table[0, 0] = -14.0
    table[7, 7] = 14.0
    return table.astype(np.float32)


def split_bf16(value):
    high = value.astype(jnp.bfloat16)
    return high, (value - high.astype(jnp.float32)).astype(jnp.bfloat16)


def derivative_tables(width):
    table = lobatto_table() * np.float32(time_step)
    along_x = np.kron(np.eye(width // 8, dtype=np.float32), table)
    high = along_x.astype(jnp.bfloat16)
    low = (along_x - high.astype(np.float32)).astype(jnp.bfloat16)
    product = np.zeros((2 * width, 2 * width), jnp.bfloat16)
    product[:width, :width] = high
    product[width:, :width] = high
    product[:width, width:] = low
    along_y = np.zeros((8, 8, width), np.float32)
    for shift in range(8):
        for node in range(8):
            along_y[shift, node, :] = table[(node - shift) % 8, node]
    return jnp.asarray(product), jnp.asarray(along_y)


def triangle_tiles(windows):
    last = 2 * windows
    width = 8 * last
    tiles = []
    for step in range(1, windows + 1):
        for kind in (0, 1):
            cut = 8 * (last - step)
            tiles.append(
                [
                    (block_of(windows, step, kind), 0, cut),
                    (block_of(windows, last + 1 - step, kind), cut, width - cut),
                ]
            )
    tiles.append([((windows - 1, 4), 0, width)])
    tiles.append([((windows - 1, 5), 0, width)])
    for window in range(windows - 2, windows // 2 - 1, -1):
        for member in (4, 5):
            cut = 16 * (window + 1)
            tiles.append(
                [((window, member), 0, cut), ((windows - 2 - window, member), cut, width - cut)]
            )
    middle = windows // 2 - 1
    cut = 16 * (middle + 1)
    tiles.append([((middle, 4), 0, cut), ((middle, 5), cut, width - cut)])
    return tiles


def block_of(windows, step, kind):
    return (windows - 1 - (step - 1) // 2, 2 * kind + (step % 2))


def diamond_tiles(windows):
    last = 2 * windows
    tiles = []

    def fill(blocks):
        offset = 0
        tile = []
        for block, elements in blocks:
            tile.append((block, offset, 8 * elements))
            offset += 8 * elements
        tiles.append(tile)

    for kind in (0, 1):
        for step in range(1, windows // 2):
            group = (step, windows - step, last - step, windows + step)
            fill([(block_of(windows, n, kind), min(n, last - n)) for n in group])
        group = (windows // 2, last - windows // 2, windows)
        fill([(block_of(windows, n, kind), min(n, last - n)) for n in group])

    def forcing_elements(window):
        step = 2 * (windows - 1 - window) + 1
        return min(step - 1, last + 1 - step)

    for member in (4, 5):
        for group in ((6, 4, 3), (5, 2, 1, 0)):
            fill([((window, member), forcing_elements(window)) for window in group])
    return tiles


def places(tiles):
    found = {}
    for index, tile in enumerate(tiles):
        for block, offset, _ in tile:
            found[block] = (index, offset)
    return found


def layer_here():
    return lax.axis_index("space") // (lax.axis_size("space") // 2)


def slot_of(windows, window):
    return jnp.bitwise_xor(window, layer_here() * (windows // 2))


def columns_at(col, offset, columns, high):
    width = col.shape[-1]
    if high:
        offset = width - offset - columns
    return (col >= offset) & (col < offset + columns)


def pack_tiles(own_ref, layout, high, out_ref):
    width = own_ref.shape[3]
    col = lax.broadcasted_iota(jnp.int32, own_ref.shape[2:], 1)
    for index, tile in enumerate(layout):
        value = None
        for block, offset, columns in tile:
            one = own_ref[slot_of(own_ref.shape[0], block[0]), block[1]]
            if offset:
                one = pltpu.roll(one, width - offset if high else offset, 1)
            if value is None:
                value = one
            else:
                value = jnp.where(columns_at(col, offset, columns, high), one, value)
        out_ref[index] = value


def pack_sides(layout, own_ref, even_ref, odd_ref):
    odd_place = lax.axis_index("space") % 2 == 1

    @pl.when(odd_place)
    def _():
        pack_tiles(own_ref, layout, False, even_ref)
        pack_tiles(own_ref, layout, True, odd_ref)

    @pl.when(jnp.logical_not(odd_place))
    def _():
        pack_tiles(own_ref, layout, True, even_ref)
        pack_tiles(own_ref, layout, False, odd_ref)


def pack_relay_kernel(own_ref, first_ref, second_ref):
    windows = own_ref.shape[0]
    cut = first_ref.shape[0]
    odd_place = lax.axis_index("space") % 2 == 1
    in_lower = lax.axis_index("tm") < windows

    def pack(high):
        layout = triangle_tiles(windows)
        pack_tiles(own_ref, layout[:cut], high, first_ref)
        pack_tiles(own_ref, layout[cut:], high, second_ref)

    @pl.when(jnp.logical_and(in_lower, odd_place))
    def _():
        pack(True)

    @pl.when(jnp.logical_and(in_lower, jnp.logical_not(odd_place)))
    def _():
        pack(False)


def pack_lower_kernel(own_ref, b1_ref, b2_ref, b3_ref, b4_ref, even_ref, odd_ref):
    windows = own_ref.shape[0]

    @pl.when(lax.axis_index("tm") < windows)
    def _():
        pack_sides(triangle_tiles(windows), own_ref, even_ref, odd_ref)


def pack_upper_kernel(own_ref, along_x_ref, along_y_ref, even_ref, odd_ref):
    windows, _, rows, width = own_ref.shape
    odd_place = lax.axis_index("space") % 2 == 1

    @pl.when(lax.axis_index("tm") >= windows)
    def _():
        layout = diamond_tiles(windows)
        pack_sides(layout, own_ref, even_ref, odd_ref)
        along_x = along_x_ref[...]
        along_y = [along_y_ref[shift] for shift in range(8)]
        col = lax.broadcasted_iota(jnp.int32, (2 * rows, width), 1)

        def tile(window, index):
            return own_ref[slot_of(windows, window), index].reshape(1, rows // 8, 8, width)

        field = None
        low = high = None
        for step in range(1, windows + 1):
            window = windows - 1 - (step - 1) // 2
            if step % 2:
                forcing = jnp.concatenate([tile(window, 4), tile(window, 5)], axis=1)
                field = forcing if field is None else field + forcing
            here = field.reshape(2 * rows, width)
            if step == 1:
                low = high = here
            else:
                shift = 8 * (step - 1)
                wanted = columns_at(col, 2 * shift, 16, False)
                low = jnp.where(wanted, pltpu.roll(here, shift, 1), low)
                wanted = columns_at(col, 2 * shift, 16, True)
                high = jnp.where(wanted, pltpu.roll(here, width - shift, 1), high)
            if step < windows:
                field = adjoint_step(
                    field, tile(window, step % 2), tile(window, 2 + step % 2), along_x, along_y
                )
        first = len(layout)
        to_even = jnp.where(odd_place, low, high)
        to_odd = jnp.where(odd_place, high, low)
        even_ref[first] = to_even[:rows]
        even_ref[first + 1] = to_even[rows:]
        odd_ref[first] = to_odd[:rows]
        odd_ref[first + 1] = to_odd[rows:]


def shift_tiles(tiles, distance):
    distance %= tiles.shape[0]
    if distance == 0:
        return tiles
    return jnp.concatenate([tiles[-distance:], tiles[:-distance]], axis=0)


def roll_columns(value, distance):
    width = value.shape[-1]
    return pltpu.roll(value.reshape(-1, width), distance % width, 1).reshape(value.shape)


def roll_nodes(value, distance):
    width = value.shape[-1]
    return pltpu.roll(value.reshape(-1, 8, width), distance % 8, 1).reshape(value.shape)


def adjoint_step(field, wind_x, wind_y, along_x, along_y):
    count, blocks, _, width = field.shape
    elements = blocks // 2
    col = lax.broadcasted_iota(jnp.int32, (1, 1, 8, width), 3)
    node = lax.broadcasted_iota(jnp.int32, (1, 1, 8, width), 2)

    from_west = roll_columns(field, 1)
    from_east = roll_columns(field, -1)
    west = jnp.where(col == 0, shift_tiles(from_west, 1), from_west)
    east = jnp.where(col == width - 1, shift_tiles(from_east, -1), from_east)
    q = 0.5 * (field + jnp.where(col % 8 == 0, west, jnp.where(col % 8 == 7, east, field)))

    down = roll_nodes(q, 1)
    up = roll_nodes(q, -1)
    before = []
    after = []
    for first in range(0, blocks, elements):
        end = first + elements
        before += [q[:, first : first + 1], down[:, first : end - 1]]
        after += [up[:, first + 1 : end], q[:, end - 1 : end]]
    before = jnp.concatenate(before, axis=1)
    after = jnp.concatenate(after, axis=1)
    q = 0.5 * (q + jnp.where(node == 0, before, jnp.where(node == 7, after, q)))

    flux_x = (jnp.concatenate([wind_x, wind_x], axis=1) * q).reshape(-1, width)
    high, low = split_bf16(flux_x)
    grad_x = jnp.dot(
        jnp.concatenate([high, low], axis=1), along_x, preferred_element_type=jnp.float32
    )
    grad_x = (grad_x[:, :width] + grad_x[:, width:]).reshape(q.shape)

    flux_y = (jnp.concatenate([wind_y, wind_y], axis=1) * q).reshape(-1, 8, width)
    grad_y = along_y[0] * flux_y
    for shift in range(1, 8):
        grad_y = grad_y + along_y[shift] * pltpu.roll(flux_y, shift, 1)
    return q - (grad_x + grad_y.reshape(q.shape))


def sweep(
    own_ref, even_ref, odd_ref, far_refs, along_x_ref, along_y_ref, start, out_ref, upper
):
    windows, _, rows, width = own_ref.shape
    layout = diamond_tiles(windows) if upper else triangle_tiles(windows)
    found = places(layout)
    odd_place = lax.axis_index("space") % 2 == 1
    along_x = along_x_ref[...]
    along_y = [along_y_ref[shift] for shift in range(8)]
    col = lax.broadcasted_iota(jnp.int32, (rows, width), 1)
    col_tile = lax.broadcasted_iota(jnp.int32, (1, 1, 8, width), 3)

    def sides(tile, shift):
        by_even = even_ref[tile]
        by_odd = odd_ref[tile]
        first = 0
        for far_ref in far_refs:
            if first <= tile < first + far_ref.shape[0]:
                by_odd = by_odd + far_ref[tile - first]
            first += far_ref.shape[0]
        west = jnp.where(odd_place, by_even, by_odd)
        east = jnp.where(odd_place, by_odd, by_even)
        if shift:
            west = pltpu.roll(west, shift, 1)
            east = pltpu.roll(east, width - shift, 1)
        return east, west

    def tiles(window, index, merged):
        own = own_ref[slot_of(windows, window), index]
        if (window, index) in found:
            east, west = sides(*found[(window, index)])
        else:
            east = west = jnp.zeros_like(own)
        if merged:
            parts = [own, jnp.where(col < width // 2, east, west)]
        else:
            parts = [own, east, west]
        return jnp.stack(parts).reshape(len(parts), rows // 8, 8, width)

    def with_finished(field, step):
        shift = 8 * (step - 1)
        pairs = [sides(len(layout) + member, shift) for member in (0, 1)]
        east = jnp.stack([pair[0] for pair in pairs]).reshape(1, 2 * rows // 8, 8, width)
        west = jnp.stack([pair[1] for pair in pairs]).reshape(1, 2 * rows // 8, 8, width)
        east = jnp.where(columns_at(col_tile, shift, 16, False), east, field[1:2])
        west = jnp.where(columns_at(col_tile, shift, 16, True), west, field[2:3])
        return jnp.concatenate([field[0:1], east, west], axis=0)

    moved = start
    for window in range(windows - 1, -1, -1):
        merged = window < windows // 2
        field = jnp.concatenate([tiles(window, 4, merged), tiles(window, 5, merged)], axis=1)
        if moved is not None:
            if moved.shape[0] > field.shape[0]:
                side = jnp.where(col_tile < width // 2, moved[1:2], moved[2:3])
                moved = jnp.concatenate([moved[0:1], side], axis=0)
            field = field + moved
        here = field[0].reshape(2 * rows, width)
        slot = slot_of(windows, window)
        out_ref[slot, 0] = here[:rows]
        out_ref[slot, 1] = here[rows:]
        if window == 0 and not upper:
            return None
        for substep in (1, 0):
            step = 2 * (windows - window) - substep
            if upper and step <= windows:
                field = with_finished(field, step)
            field = adjoint_step(
                field,
                tiles(window, substep, merged),
                tiles(window, 2 + substep, merged),
                along_x,
                along_y,
            )
        moved = field
    return moved[0].reshape(2 * rows, width)


def upper_kernel(
    own_ref,
    odd_ref,
    even_ref,
    b1_ref,
    b2_ref,
    along_x_ref,
    along_y_ref,
    out_ref,
    sent_ref,
):
    windows = own_ref.shape[0]

    @pl.when(lax.axis_index("tm") >= windows)
    def _():
        sent_ref[...] = sweep(
            own_ref, even_ref, odd_ref, (), along_x_ref, along_y_ref, None, out_ref, True
        )


def lower_kernel(
    done_ref,
    own_ref,
    even_ref,
    odd_ref,
    far_x_ref,
    far_y_ref,
    along_x_ref,
    along_y_ref,
    here_ref,
    pe_ref,
    po_ref,
    out_ref,
):
    windows, _, rows, width = own_ref.shape

    @pl.when(lax.axis_index("tm") < windows)
    def _():
        odd_place = lax.axis_index("space") % 2 == 1
        by_even = pe_ref[...]
        by_odd = po_ref[...]
        west = jnp.where(odd_place, by_even, by_odd)
        east = jnp.where(odd_place, by_odd, by_even)
        far_refs = (far_x_ref, far_y_ref)
        start = jnp.stack([here_ref[...], east, west]).reshape(3, 2 * rows // 8, 8, width)
        sweep(
            own_ref, even_ref, odd_ref, far_refs, along_x_ref, along_y_ref, start, out_ref, False
        )


def local_call(kernel, out_shape, in_specs, out_specs=None, **options):
    whole = pl.BlockSpec(memory_space=pltpu.VMEM)
    if isinstance(in_specs, int):
        in_specs = [whole] * in_specs
    return pl.pallas_call(
        kernel,
        out_shape=out_shape,
        in_specs=in_specs,
        out_specs=out_specs or jax.tree.map(lambda _: whole, out_shape),
        compiler_params=pltpu.CompilerParams(vmem_limit_bytes=32 * 1024 * 1024),
        **options,
    )


def on_device(forcing, wind_x, wind_y):
    members, _, levels, rows, width = forcing.shape
    tm = lax.axis_size("tm")
    space = lax.axis_size("space")
    group = levels
    layer = space // 2
    anything = pl.BlockSpec(memory_space=pl.ANY)

    def same(t, s):
        return t, s

    def even_mate(t, s):
        return t, s ^ 1

    def is_far(s):
        return s % layer in (0, layer - 1)

    def odd_mate(t, s):
        mate = (s + 1) % space if s % 2 else (s - 1) % space
        return (t ^ (group // 2) if is_far(s) else t), mate

    def along_y_mate(t, s):
        row = max(2, layer // 4)
        return t, (s + row if s % layer == 0 else s - row)

    def exchange(block, mate, chosen, dt=0):
        pairs = []
        for t in range(tm):
            for s in range(space):
                if chosen(t, s):
                    to_t, to_s = mate(t, s)
                    pairs.append((t * space + s, (to_t + dt) * space + to_s))
        return lax.ppermute(block, ("tm", "space"), pairs)

    def upper(t, s):
        return t >= group

    groups = []
    for s in range(space):
        flip = (s // layer) * (group // 2)
        for first in range(0, tm, group):
            groups.append([(first + (place ^ flip)) * space + s for place in range(group)])

    def within_groups(block):
        return lax.all_to_all(
            block, ("tm", "space"), 0, 0, axis_index_groups=groups, tiled=True
        )

    packed = jnp.concatenate([wind_x[0], wind_y[0], forcing[:, 0]], axis=0)
    own = within_groups(jnp.swapaxes(packed, 0, 1))

    whole = pl.BlockSpec(memory_space=pltpu.VMEM)
    anything = pl.BlockSpec(memory_space=pl.ANY)
    along_x, along_y = derivative_tables(width)

    def tiles(number):
        return jax.ShapeDtypeStruct((number, rows, width), jnp.float32)

    def lower(t, s):
        return not upper(t, s)

    diamond = tiles(len(diamond_tiles(group)) + 2)
    triangle = tiles(len(triangle_tiles(group)))
    to_even, to_odd = local_call(pack_upper_kernel, (diamond, diamond), 3)(own, along_x, along_y)
    upper_odd = exchange(to_odd, odd_mate, upper)
    upper_even = exchange(to_even, even_mate, upper)

    cut = (len(triangle_tiles(group)) + 1) // 2
    halves = tiles(cut), tiles(len(triangle_tiles(group)) - cut)
    first_half, second_half = local_call(pack_relay_kernel, halves, 1)(own)

    def relay(block, neighbour):
        there = exchange(block, neighbour, lambda t, s: is_far(s) and lower(t, s))
        pairs = []
        for t in range(group):
            for s in range(space):
                if is_far(s):
                    from_t, from_s = neighbour(t, s)
                    to_t, to_s = odd_mate(t, s)
                    pairs.append((from_t * space + from_s, to_t * space + to_s))
        return there, lax.ppermute(there, ("tm", "space"), pairs)

    there_x, far_x = relay(first_half, even_mate)
    there_y, far_y = relay(second_half, along_y_mate)
    to_even, to_odd = local_call(
        pack_lower_kernel, (triangle, triangle), [whole] + [anything] * 4
    )(own, upper_odd, upper_even, there_x, there_y)
    lower_odd = exchange(to_odd, odd_mate, lambda t, s: lower(t, s) and not is_far(s))
    lower_even = exchange(to_even, even_mate, lower)

    result_shape = jax.ShapeDtypeStruct((group, members, rows, width), jnp.float32)
    flat_field = jax.ShapeDtypeStruct((members * rows, width), jnp.float32)
    done, sent = local_call(
        upper_kernel,
        (result_shape, flat_field),
        [whole] * 3 + [anything] * 2 + [whole] * 2,
    )(own, upper_odd, upper_even, lower_odd, lower_even, along_x, along_y)
    from_here = exchange(sent, same, upper, -group)
    from_even = exchange(sent, even_mate, upper, -group)
    from_odd = exchange(sent, odd_mate, upper, -group)
    result = local_call(lower_kernel, result_shape, 11, input_output_aliases={0: 0})(
        done, own, lower_even, lower_odd, far_x, far_y, along_x, along_y, from_here, from_even, from_odd
    )
    result = within_groups(result)
    return jnp.swapaxes(result, 0, 1)[:, None]


def solution(mesh):
    placed = (
        P(None, "tm", None, None, "space"),
        P("tm", None, None, None, "space"),
        P("tm", None, None, None, "space"),
    )
    return jax.shard_map(
        on_device,
        mesh=mesh,
        in_specs=placed,
        out_specs=P(None, "tm", None, None, "space"),
        check_vma=False,
    )
```

```python
import jax
import jax.numpy as jnp
import numpy as np
from jax import lax
from jax.experimental import pallas as pl
from jax.experimental.pallas import tpu as pltpu
from jax.sharding import PartitionSpec as P

time_step = 0.01
lobatto_points = [
    -1.0,
    -0.8717401485096066,
    -0.5917001814331423,
    -0.20929921790247888,
    0.20929921790247888,
    0.5917001814331423,
    0.8717401485096066,
    1.0,
]


def legendre_seven(point):
    before = 1.0
    current = point
    for order in range(1, 7):
        before, current = (
            current,
            ((2 * order + 1) * point * current - order * before) / (order + 1),
        )
    return current


def lobatto_table():
    values = [legendre_seven(point) for point in lobatto_points]
    table = np.zeros((8, 8))
    for row_index in range(8):
        for col_index in range(8):
            if row_index != col_index:
                table[row_index, col_index] = values[row_index] / (
                    values[col_index] * (lobatto_points[row_index] - lobatto_points[col_index])
                )
    table[0, 0] = -14.0
    table[7, 7] = 14.0
    return table.astype(np.float32)


def split_bf16(value):
    high = value.astype(jnp.bfloat16)
    return high, (value - high.astype(jnp.float32)).astype(jnp.bfloat16)


def derivative_tables(width):
    table = lobatto_table() * np.float32(time_step)
    along_x = np.kron(np.eye(width // 8, dtype=np.float32), table)
    high = along_x.astype(jnp.bfloat16)
    low = (along_x - high.astype(np.float32)).astype(jnp.bfloat16)
    product = np.zeros((2 * width, 2 * width), jnp.bfloat16)
    product[:width, :width] = high
    product[width:, :width] = high
    product[:width, width:] = low
    along_y = np.zeros((8, 8, width), np.float32)
    for shift in range(8):
        for node in range(8):
            along_y[shift, node, :] = table[(node - shift) % 8, node]
    return jnp.asarray(product), jnp.asarray(along_y)


def triangle_tiles(windows):
    last = 2 * windows
    width = 8 * last
    tiles = []
    for step in range(1, windows + 1):
        for kind in (0, 1):
            cut = 8 * (last - step)
            tiles.append(
                [
                    (block_of(windows, step, kind), 0, cut),
                    (block_of(windows, last + 1 - step, kind), cut, width - cut),
                ]
            )
    tiles.append([((windows - 1, 4), 0, width)])
    tiles.append([((windows - 1, 5), 0, width)])
    for window in range(windows - 2, windows // 2 - 1, -1):
        for member in (4, 5):
            cut = 16 * (window + 1)
            tiles.append(
                [((window, member), 0, cut), ((windows - 2 - window, member), cut, width - cut)]
            )
    middle = windows // 2 - 1
    cut = 16 * (middle + 1)
    tiles.append([((middle, 4), 0, cut), ((middle, 5), cut, width - cut)])
    return tiles


def block_of(windows, step, kind):
    return (windows - 1 - (step - 1) // 2, 2 * kind + (step % 2))


def diamond_tiles(windows):
    last = 2 * windows
    tiles = []

    def fill(blocks):
        offset = 0
        tile = []
        for block, elements in blocks:
            tile.append((block, offset, 8 * elements))
            offset += 8 * elements
        tiles.append(tile)

    for kind in (0, 1):
        for step in range(1, windows // 2):
            group = (step, windows - step, last - step, windows + step)
            fill([(block_of(windows, n, kind), min(n, last - n)) for n in group])
        group = (windows // 2, last - windows // 2, windows)
        fill([(block_of(windows, n, kind), min(n, last - n)) for n in group])

    def forcing_elements(window):
        step = 2 * (windows - 1 - window) + 1
        return min(step - 1, last + 1 - step)

    for member in (4, 5):
        for group in ((6, 4, 3), (5, 2, 1, 0)):
            fill([((window, member), forcing_elements(window)) for window in group])
    return tiles


def places(tiles):
    found = {}
    for index, tile in enumerate(tiles):
        for block, offset, _ in tile:
            found[block] = (index, offset)
    return found


def layer_here():
    return lax.axis_index("space") // (lax.axis_size("space") // 2)


def slot_of(windows, window):
    return jnp.bitwise_xor(window, layer_here() * (windows // 2))


def columns_at(col, offset, columns, high):
    width = col.shape[-1]
    if high:
        offset = width - offset - columns
    return (col >= offset) & (col < offset + columns)


def pack_tiles(own_ref, layout, high, out_ref):
    width = own_ref.shape[3]
    col = lax.broadcasted_iota(jnp.int32, own_ref.shape[2:], 1)
    for index, tile in enumerate(layout):
        value = None
        for block, offset, columns in tile:
            one = own_ref[slot_of(own_ref.shape[0], block[0]), block[1]]
            if offset:
                one = pltpu.roll(one, width - offset if high else offset, 1)
            if value is None:
                value = one
            else:
                value = jnp.where(columns_at(col, offset, columns, high), one, value)
        out_ref[index] = value


def pack_sides(layout, own_ref, even_ref, odd_ref):
    odd_place = lax.axis_index("space") % 2 == 1

    @pl.when(odd_place)
    def _():
        pack_tiles(own_ref, layout, False, even_ref)
        pack_tiles(own_ref, layout, True, odd_ref)

    @pl.when(jnp.logical_not(odd_place))
    def _():
        pack_tiles(own_ref, layout, True, even_ref)
        pack_tiles(own_ref, layout, False, odd_ref)


def pack_relay_kernel(own_ref, through_ref, first_ref, second_ref, out_ref):
    windows = own_ref.shape[0]
    cut = first_ref.shape[0]
    odd_place = lax.axis_index("space") % 2 == 1
    in_lower = lax.axis_index("tm") < windows

    def pack(high):
        layout = triangle_tiles(windows)
        pack_tiles(own_ref, layout[:cut], high, first_ref)
        pack_tiles(own_ref, layout[cut:], high, second_ref)

    @pl.when(jnp.logical_and(in_lower, odd_place))
    def _():
        pack(True)

    @pl.when(jnp.logical_and(in_lower, jnp.logical_not(odd_place)))
    def _():
        pack(False)


def pack_lower_kernel(own_ref, b1_ref, b2_ref, b3_ref, even_ref, odd_ref, x_ref, y_ref):
    windows = own_ref.shape[0]

    @pl.when(lax.axis_index("tm") < windows)
    def _():
        pack_sides(triangle_tiles(windows), own_ref, even_ref, odd_ref)


def pack_upper_kernel(own_ref, along_x_ref, along_y_ref, even_ref, odd_ref):
    windows, _, rows, width = own_ref.shape
    odd_place = lax.axis_index("space") % 2 == 1

    @pl.when(lax.axis_index("tm") >= windows)
    def _():
        layout = diamond_tiles(windows)
        pack_sides(layout, own_ref, even_ref, odd_ref)
        along_x = along_x_ref[...]
        along_y = [along_y_ref[shift] for shift in range(8)]
        col = lax.broadcasted_iota(jnp.int32, (2 * rows, width), 1)

        def tile(window, index):
            return own_ref[slot_of(windows, window), index].reshape(1, rows // 8, 8, width)

        field = None
        low = high = None
        for step in range(1, windows + 1):
            window = windows - 1 - (step - 1) // 2
            if step % 2:
                forcing = jnp.concatenate([tile(window, 4), tile(window, 5)], axis=1)
                field = forcing if field is None else field + forcing
            here = field.reshape(2 * rows, width)
            if step == 1:
                low = high = here
            else:
                shift = 8 * (step - 1)
                wanted = columns_at(col, 2 * shift, 16, False)
                low = jnp.where(wanted, pltpu.roll(here, shift, 1), low)
                wanted = columns_at(col, 2 * shift, 16, True)
                high = jnp.where(wanted, pltpu.roll(here, width - shift, 1), high)
            if step < windows:
                field = adjoint_step(
                    field, tile(window, step % 2), tile(window, 2 + step % 2), along_x, along_y
                )
        first = len(layout)
        to_even = jnp.where(odd_place, low, high)
        to_odd = jnp.where(odd_place, high, low)
        even_ref[first] = to_even[:rows]
        even_ref[first + 1] = to_even[rows:]
        odd_ref[first] = to_odd[:rows]
        odd_ref[first + 1] = to_odd[rows:]


def shift_tiles(tiles, distance):
    distance %= tiles.shape[0]
    if distance == 0:
        return tiles
    return jnp.concatenate([tiles[-distance:], tiles[:-distance]], axis=0)


def roll_columns(value, distance):
    width = value.shape[-1]
    return pltpu.roll(value.reshape(-1, width), distance % width, 1).reshape(value.shape)


def roll_nodes(value, distance):
    width = value.shape[-1]
    return pltpu.roll(value.reshape(-1, 8, width), distance % 8, 1).reshape(value.shape)


def adjoint_step(field, wind_x, wind_y, along_x, along_y):
    count, blocks, _, width = field.shape
    elements = blocks // 2
    col = lax.broadcasted_iota(jnp.int32, (1, 1, 8, width), 3)
    node = lax.broadcasted_iota(jnp.int32, (1, 1, 8, width), 2)

    from_west = roll_columns(field, 1)
    from_east = roll_columns(field, -1)
    west = jnp.where(col == 0, shift_tiles(from_west, 1), from_west)
    east = jnp.where(col == width - 1, shift_tiles(from_east, -1), from_east)
    q = 0.5 * (field + jnp.where(col % 8 == 0, west, jnp.where(col % 8 == 7, east, field)))

    down = roll_nodes(q, 1)
    up = roll_nodes(q, -1)
    before = []
    after = []
    for first in range(0, blocks, elements):
        end = first + elements
        before += [q[:, first : first + 1], down[:, first : end - 1]]
        after += [up[:, first + 1 : end], q[:, end - 1 : end]]
    before = jnp.concatenate(before, axis=1)
    after = jnp.concatenate(after, axis=1)
    q = 0.5 * (q + jnp.where(node == 0, before, jnp.where(node == 7, after, q)))

    flux_x = (jnp.concatenate([wind_x, wind_x], axis=1) * q).reshape(-1, width)
    high, low = split_bf16(flux_x)
    grad_x = jnp.dot(
        jnp.concatenate([high, low], axis=1), along_x, preferred_element_type=jnp.float32
    )
    grad_x = (grad_x[:, :width] + grad_x[:, width:]).reshape(q.shape)

    flux_y = (jnp.concatenate([wind_y, wind_y], axis=1) * q).reshape(-1, 8, width)
    grad_y = along_y[0] * flux_y
    for shift in range(1, 8):
        grad_y = grad_y + along_y[shift] * pltpu.roll(flux_y, shift, 1)
    return q - (grad_x + grad_y.reshape(q.shape))


def sweep(
    own_ref, even_ref, odd_ref, far_refs, along_x_ref, along_y_ref, start, out_ref, upper
):
    windows, _, rows, width = own_ref.shape
    layout = diamond_tiles(windows) if upper else triangle_tiles(windows)
    found = places(layout)
    odd_place = lax.axis_index("space") % 2 == 1
    along_x = along_x_ref[...]
    along_y = [along_y_ref[shift] for shift in range(8)]
    col = lax.broadcasted_iota(jnp.int32, (rows, width), 1)
    col_tile = lax.broadcasted_iota(jnp.int32, (1, 1, 8, width), 3)

    def sides(tile, shift):
        by_even = even_ref[tile]
        by_odd = odd_ref[tile]
        first = 0
        for far_ref in far_refs:
            if first <= tile < first + far_ref.shape[0]:
                by_odd = by_odd + far_ref[tile - first]
            first += far_ref.shape[0]
        west = jnp.where(odd_place, by_even, by_odd)
        east = jnp.where(odd_place, by_odd, by_even)
        if shift:
            west = pltpu.roll(west, shift, 1)
            east = pltpu.roll(east, width - shift, 1)
        return east, west

    def tiles(window, index, merged):
        own = own_ref[slot_of(windows, window), index]
        if (window, index) in found:
            east, west = sides(*found[(window, index)])
        else:
            east = west = jnp.zeros_like(own)
        if merged:
            parts = [own, jnp.where(col < width // 2, east, west)]
        else:
            parts = [own, east, west]
        return jnp.stack(parts).reshape(len(parts), rows // 8, 8, width)

    def with_finished(field, step):
        shift = 8 * (step - 1)
        pairs = [sides(len(layout) + member, shift) for member in (0, 1)]
        east = jnp.stack([pair[0] for pair in pairs]).reshape(1, 2 * rows // 8, 8, width)
        west = jnp.stack([pair[1] for pair in pairs]).reshape(1, 2 * rows // 8, 8, width)
        east = jnp.where(columns_at(col_tile, shift, 16, False), east, field[1:2])
        west = jnp.where(columns_at(col_tile, shift, 16, True), west, field[2:3])
        return jnp.concatenate([field[0:1], east, west], axis=0)

    moved = start
    for window in range(windows - 1, -1, -1):
        merged = window < windows // 2
        field = jnp.concatenate([tiles(window, 4, merged), tiles(window, 5, merged)], axis=1)
        if moved is not None:
            if moved.shape[0] > field.shape[0]:
                side = jnp.where(col_tile < width // 2, moved[1:2], moved[2:3])
                moved = jnp.concatenate([moved[0:1], side], axis=0)
            field = field + moved
        here = field[0].reshape(2 * rows, width)
        slot = slot_of(windows, window)
        out_ref[slot, 0] = here[:rows]
        out_ref[slot, 1] = here[rows:]
        if window == 0 and not upper:
            return None
        for substep in (1, 0):
            step = 2 * (windows - window) - substep
            if upper and step <= windows:
                field = with_finished(field, step)
            field = adjoint_step(
                field,
                tiles(window, substep, merged),
                tiles(window, 2 + substep, merged),
                along_x,
                along_y,
            )
        moved = field
    return moved[0].reshape(2 * rows, width)


def upper_kernel(
    own_ref,
    odd_ref,
    even_ref,
    along_x_ref,
    along_y_ref,
    out_ref,
    sent_ref,
):
    windows = own_ref.shape[0]

    @pl.when(lax.axis_index("tm") >= windows)
    def _():
        sent_ref[...] = sweep(
            own_ref, even_ref, odd_ref, (), along_x_ref, along_y_ref, None, out_ref, True
        )


def pass_kernel(sent_ref, b1_ref, b2_ref, out_ref):
    pass


def lower_kernel(
    done_ref,
    own_ref,
    even_ref,
    odd_ref,
    far_x_ref,
    far_y_ref,
    along_x_ref,
    along_y_ref,
    here_ref,
    pe_ref,
    po_ref,
    out_ref,
):
    windows, _, rows, width = own_ref.shape

    @pl.when(lax.axis_index("tm") < windows)
    def _():
        odd_place = lax.axis_index("space") % 2 == 1
        by_even = pe_ref[...]
        by_odd = po_ref[...]
        west = jnp.where(odd_place, by_even, by_odd)
        east = jnp.where(odd_place, by_odd, by_even)
        far_refs = (far_x_ref, far_y_ref)
        start = jnp.stack([here_ref[...], east, west]).reshape(3, 2 * rows // 8, 8, width)
        sweep(
            own_ref, even_ref, odd_ref, far_refs, along_x_ref, along_y_ref, start, out_ref, False
        )


def local_call(kernel, out_shape, in_specs, out_specs=None, **options):
    whole = pl.BlockSpec(memory_space=pltpu.VMEM)
    if isinstance(in_specs, int):
        in_specs = [whole] * in_specs
    return pl.pallas_call(
        kernel,
        out_shape=out_shape,
        in_specs=in_specs,
        out_specs=out_specs or jax.tree.map(lambda _: whole, out_shape),
        compiler_params=pltpu.CompilerParams(vmem_limit_bytes=32 * 1024 * 1024),
        **options,
    )


def on_device(forcing, wind_x, wind_y):
    members, _, levels, rows, width = forcing.shape
    tm = lax.axis_size("tm")
    space = lax.axis_size("space")
    group = levels
    layer = space // 2
    anything = pl.BlockSpec(memory_space=pl.ANY)

    def same(t, s):
        return t, s

    def even_mate(t, s):
        return t, s ^ 1

    def is_far(s):
        return s % layer in (0, layer - 1)

    def odd_mate(t, s):
        mate = (s + 1) % space if s % 2 else (s - 1) % space
        return (t ^ (group // 2) if is_far(s) else t), mate

    def along_y_mate(t, s):
        row = max(2, layer // 4)
        return t, (s + row if s % layer == 0 else s - row)

    def exchange(block, mate, chosen, dt=0):
        pairs = []
        for t in range(tm):
            for s in range(space):
                if chosen(t, s):
                    to_t, to_s = mate(t, s)
                    pairs.append((t * space + s, (to_t + dt) * space + to_s))
        return lax.ppermute(block, ("tm", "space"), pairs)

    def upper(t, s):
        return t >= group

    groups = []
    for s in range(space):
        flip = (s // layer) * (group // 2)
        for first in range(0, tm, group):
            groups.append([(first + (place ^ flip)) * space + s for place in range(group)])

    def within_groups(block):
        return lax.all_to_all(
            block, ("tm", "space"), 0, 0, axis_index_groups=groups, tiled=True
        )

    packed = jnp.concatenate([wind_x[0], wind_y[0], forcing[:, 0]], axis=0)
    own = within_groups(jnp.swapaxes(packed, 0, 1))

    whole = pl.BlockSpec(memory_space=pltpu.VMEM)
    anything = pl.BlockSpec(memory_space=pl.ANY)
    along_x, along_y = derivative_tables(width)

    def tiles(number):
        return jax.ShapeDtypeStruct((number, rows, width), jnp.float32)

    def lower(t, s):
        return not upper(t, s)

    diamond = tiles(len(diamond_tiles(group)) + 2)
    triangle = tiles(len(triangle_tiles(group)))
    to_even, to_odd = local_call(pack_upper_kernel, (diamond, diamond), 3)(own, along_x, along_y)
    upper_odd = exchange(to_odd, odd_mate, upper)

    cut = (len(triangle_tiles(group)) + 1) // 2
    halves = tiles(cut), tiles(len(triangle_tiles(group)) - cut)
    first_half, second_half, to_even = local_call(
        pack_relay_kernel, halves + (diamond,), 2, input_output_aliases={1: 2}
    )(own, to_even)
    upper_even = exchange(to_even, even_mate, upper)

    def relay(block, neighbour):
        return exchange(block, neighbour, lambda t, s: is_far(s) and lower(t, s))

    def send_on(there, neighbour):
        pairs = []
        for t in range(group):
            for s in range(space):
                if is_far(s):
                    from_t, from_s = neighbour(t, s)
                    to_t, to_s = odd_mate(t, s)
                    pairs.append((from_t * space + from_s, to_t * space + to_s))
        return lax.ppermute(there, ("tm", "space"), pairs)

    there_x = relay(first_half, even_mate)
    there_y = relay(second_half, along_y_mate)
    to_even, to_odd, there_x, there_y = local_call(
        pack_lower_kernel,
        (triangle, triangle) + halves,
        [whole, anything, whole, whole],
        input_output_aliases={2: 2, 3: 3},
    )(own, upper_even, there_x, there_y)
    far_x = send_on(there_x, even_mate)
    far_y = send_on(there_y, along_y_mate)
    lower_odd = exchange(to_odd, odd_mate, lambda t, s: lower(t, s) and not is_far(s))
    lower_even = exchange(to_even, even_mate, lower)

    result_shape = jax.ShapeDtypeStruct((group, members, rows, width), jnp.float32)
    flat_field = jax.ShapeDtypeStruct((members * rows, width), jnp.float32)
    done, sent = local_call(
        upper_kernel,
        (result_shape, flat_field),
        5,
        cost_estimate=pl.CostEstimate(
            flops=10**10, bytes_accessed=10**6, transcendentals=0
        ),
    )(own, upper_odd, upper_even, along_x, along_y)
    sent = local_call(
        pass_kernel, flat_field, [whole, anything, anything], input_output_aliases={0: 0}
    )(sent, lower_odd, lower_even)
    from_here = exchange(sent, same, upper, -group)
    from_even = exchange(sent, even_mate, upper, -group)
    from_odd = exchange(sent, odd_mate, upper, -group)
    result = local_call(lower_kernel, result_shape, 11, input_output_aliases={0: 0})(
        done, own, lower_even, lower_odd, far_x, far_y, along_x, along_y, from_here, from_even, from_odd
    )
    result = within_groups(result)
    return jnp.swapaxes(result, 0, 1)[:, None]


def solution(mesh):
    placed = (
        P(None, "tm", None, None, "space"),
        P("tm", None, None, None, "space"),
        P("tm", None, None, None, "space"),
    )
    return jax.shard_map(
        on_device,
        mesh=mesh,
        in_specs=placed,
        out_specs=P(None, "tm", None, None, "space"),
        check_vma=False,
    )
```
